128 devices in a mesh: lon: 16 (over x_lo, y, core), lat: 8 (over z, x_hi).
Axes of the slice: x: 4 (x_hi: 2, x_lo: 2; x = x_hi * 2 + x_lo), y: 4, z: 4, core: 2. Of those that a mesh axis runs over, the one named last changes fastest.
Arguments:
- input_field: bfloat16 [64, 512, 2048], P(None, 'lat', 'lon'), may hold values from -6 to 6
- conv_first: bfloat16 [3, 3, 128, 64], replicated, may hold values from -0.4375 to 0.4375
- conv_rest: bfloat16 [3, 3, 3, 128, 128], replicated, may hold values from -0.3125 to 0.3125
- flag_patch: int32 [8, 16, 32], P('lat', 'lon'), may hold values from 0 to 31, as said below
- flag_count: int32 [8, 16], P('lat', 'lon'), may hold values from 0 to 32, as said below
- w_embed: bfloat16 [2048, 1024], replicated, may hold values from -0.125 to 0.125
- pos_embed: bfloat16 [16, 1024], replicated, may hold values from -3 to 3
- token_mix: bfloat16 [16, 16], replicated, may hold values from -1.5 to 1.5
- w_up: bfloat16 [1024, 4096], replicated, may hold values from -0.1875 to 0.1875
- w_down: bfloat16 [4096, 1024], replicated, may hold values from -0.09375 to 0.09375
- w_head: bfloat16 [1024, 8], replicated, may hold values from -0.1875 to 0.1875
Outputs:
- features: bfloat16 [512, 2048, 128], P('lat', 'lon')
- flag_scores: float32 [8, 16, 32, 8], P('lat', 'lon')
The draws below stay inside these ranges and needn't reach their ends.
Inputs may be any that keep to these rules, and one draw needn't show every extreme that they name: `flag_patch`: within a tile the 32 entries are distinct; only the first flag_count entries of a tile are live. `flag_count`: in each latitude band the counts of the tiles sum to 256 minus 1 to 15; some tile of every band has 32.
All inputs are finite; a program needn't handle non-finite values.
Results may differ from the reference program's by a relative error of at most 0.011.
Values may be sent and summed in bfloat16 or wider, within the bound.
A program may use at most 128 MiB of HBM per device.

```python
import jax
import jax.numpy as jnp
from jax import lax

VARS = 64
CH = 128
PATCH = 16
SUB = 4
WIDTH = 1024
MLP = 4096
NCLS = 8
PLAT_DEV = 4
PLON_DEV = 8
NLAT = 512
NLON = 2048
PATCHES = 32
NTOK = 16
FEAT = 2048
FSLOT = 32
N_LON = 16
N_LAT = 8


def count_table(key):
    band_keys = jax.random.split(jax.random.fold_in(key, 11), N_LAT)

    def one_band(band_key):
        subkeys = jax.random.split(band_key, 5)
        pair_count = N_LON // 2
        largest = 2 * N_LON
        shuffled = jax.random.permutation(subkeys[0], pair_count)
        shortfall = jax.random.randint(subkeys[1], (), 1, N_LON)
        pair_index = jnp.arange(pair_count)
        totals = largest - jnp.where(pair_index == shuffled[1], shortfall, 0)
        drawn = jax.random.randint(subkeys[2], (pair_count,), 0, largest + 1)
        first_side = jnp.where(pair_index == shuffled[0], largest, drawn % (totals + 1))
        second = totals - first_side
        flipped = jax.random.randint(subkeys[3], (pair_count,), 0, 2)
        left_side = jnp.where(flipped == 1, second, first_side)
        right_side = jnp.where(flipped == 1, first_side, second)
        paired = jnp.stack([left_side, right_side], axis=1).reshape(N_LON)
        order = jax.random.permutation(subkeys[4], N_LON)
        return paired[order]
    return jax.vmap(one_band)(band_keys).astype(jnp.int32)


def draw_flag_count(key, part):
    return count_table(key)


def draw_flag_patch(key, part):
    tile_keys = jax.random.split(jax.random.fold_in(key, 23), N_LAT * N_LON)

    def pick_patches(tile_key):
        return jax.random.permutation(tile_key, PATCHES)[:FSLOT]
    return jax.vmap(pick_patches)(tile_keys).reshape(N_LAT, N_LON, FSLOT).astype(jnp.int32)


def draw_pos_embed(key, part):
    key = jax.random.fold_in(key, 37)
    values = 0.5 * jnp.clip(jax.random.normal(key, (NTOK, WIDTH), jnp.float32), -6.0, 6.0)
    return values.astype(jnp.bfloat16)


def block_levels(key, extent, cuts, smallest, high):
    level = 1.0
    for position, parts in cuts:
        steps = jax.random.uniform(jax.random.fold_in(jax.random.fold_in(key, 6), position), (parts,), jnp.float32, smallest / len(cuts), high / len(cuts))
        level = level * jnp.repeat(jnp.exp(steps), extent[position] // parts).reshape((-1,) + (1,) * (len(extent) - 1 - position))
    return level


def bell_draw(own_key, shape, width, most, cuts=(), kind=jnp.bfloat16):
    array = jax.random.normal(own_key, shape, jnp.float32) * width
    if len(cuts) > 0:
        array = block_levels(own_key, shape, cuts, -0.22, 0.18) * array
    return jnp.clip(array, min=-most, max=most).astype(kind)


def setup_inputs(seed: int = 0) -> dict:
    streams_of = jax.random.split(jax.random.key(seed), 12)
    return {
        "input_field": bell_draw(streams_of[0], (VARS, NLAT, NLON), 1.0, 6.0, ((1, 8), (2, 16))),
        "conv_first": bell_draw(streams_of[1], (3, 3, CH, VARS), (3 * VARS) ** -0.5, 0.4375),
        "conv_rest": bell_draw(streams_of[2], (3, 3, 3, CH, CH), (3 * CH) ** -0.5, 0.3125),
        "flag_patch": draw_flag_patch(jax.random.fold_in(streams_of[11], 71), 0),
        "flag_count": draw_flag_count(jax.random.fold_in(streams_of[11], 71), 0),
        "w_embed": bell_draw(streams_of[5], (FEAT, WIDTH), FEAT ** -0.5, 0.125),
        "pos_embed": draw_pos_embed(jax.random.fold_in(streams_of[11], 71), 0),
        "token_mix": bell_draw(streams_of[7], (NTOK, NTOK), NTOK ** -0.5, 1.5),
        "w_up": bell_draw(streams_of[8], (WIDTH, MLP), WIDTH ** -0.5, 0.1875),
        "w_down": bell_draw(streams_of[9], (MLP, WIDTH), MLP ** -0.5, 0.09375),
        "w_head": bell_draw(streams_of[10], (WIDTH, NCLS), WIDTH ** -0.5, 0.1875),
    }


def conv_layer(source, taps):
    padded = jnp.pad(source, ((0, 0), (1, 1), (0, 0)))
    padded = jnp.concatenate([padded[:, :, -1:], padded, padded[:, :, :1]], axis=2)
    height = source.shape[1]
    breadth = source.shape[2]
    summed = jnp.zeros((taps.shape[2], height, breadth), jnp.float32)
    for row_step in range(3):
        for col_step in range(3):
            window = padded[:, row_step:row_step + height, col_step:col_step + breadth].astype(jnp.float32)
            summed = summed + jnp.einsum('oc,cij->oij', taps[row_step, col_step].astype(jnp.float32), window)
    return jax.nn.silu(summed).astype(jnp.bfloat16)

def layer_norm(values):
    centred = values - lax.optimization_barrier(jnp.mean(values, axis=-1, keepdims=True))
    return centred * lax.rsqrt(lax.optimization_barrier(jnp.mean(centred * centred, axis=-1, keepdims=True)) + 1e-05)

def classify(selected, w_embed, pos_embed, token_mix, w_up, w_down, w_head):
    wide = jnp.float32
    tokens = (jnp.einsum('ptf,fd->ptd', selected.astype(wide), w_embed.astype(wide)) + pos_embed.astype(wide)).astype(jnp.bfloat16)
    tokens_wide = tokens.astype(wide)
    normed = layer_norm(tokens_wide).astype(jnp.bfloat16)
    mixed_tokens = (tokens_wide + jnp.einsum('ts,psd->ptd', token_mix.astype(wide), normed.astype(wide))).astype(jnp.bfloat16)
    mixed_wide = mixed_tokens.astype(wide)
    normed_two = layer_norm(mixed_wide).astype(jnp.bfloat16)
    hidden = jax.nn.gelu(jnp.einsum('ptd,dh->pth', normed_two.astype(wide), w_up.astype(wide))).astype(jnp.bfloat16)
    encoded = mixed_wide + jnp.einsum('pth,hd->ptd', hidden.astype(wide), w_down.astype(wide))
    pooled = lax.optimization_barrier(jnp.mean(layer_norm(encoded), axis=1)).astype(jnp.bfloat16)
    return jnp.dot(pooled, w_head, preferred_element_type=jnp.float32)

def reference(input_field, conv_first, conv_rest, flag_patch, flag_count, w_embed, pos_embed, token_mix, w_up, w_down, w_head):
    current = conv_layer(input_field, conv_first)
    for conv_index in range(3):
        current = conv_layer(current, conv_rest[conv_index])
    features = jnp.transpose(current, (1, 2, 0))
    per_patch = PATCH // SUB
    blocks = features.reshape(N_LAT, PLAT_DEV, per_patch, SUB, N_LON, PLON_DEV, per_patch, SUB, CH)
    blocks = blocks.transpose(0, 4, 1, 5, 2, 6, 3, 7, 8).reshape(N_LAT, N_LON, PATCHES, NTOK, FEAT)
    picked = jnp.take_along_axis(blocks, flag_patch[:, :, :, None, None], axis=2)

    def band_scores(band):
        scores = classify(band.reshape(N_LON * FSLOT, NTOK, FEAT), w_embed, pos_embed, token_mix, w_up, w_down, w_head)
        return scores.reshape(N_LON, FSLOT, NCLS)
    scores = lax.map(band_scores, picked)
    active = jnp.arange(FSLOT, dtype=jnp.int32)[None, None, :] < flag_count[:, :, None]
    flag_scores = jnp.where(active[:, :, :, None], scores, jnp.zeros_like(scores))
    return (features, flag_scores)
```

```python
import functools

import jax
import jax.numpy as jnp
from jax import lax
from jax.experimental import pallas as pl
from jax.experimental.pallas import tpu as pltpu
from jax.sharding import PartitionSpec as P

BF = jnp.bfloat16
F32 = jnp.float32
MESH = pl.DeviceIdType.MESH

W = 9
Q = W + 2
S = 16
COLS = W * S
PITCH = 152
NEG = (((1,), (1,)), ((), ()))


def halo_kernel(x_ref, p_ref, xf, fx, row_up, row_dn, colf, col_l, col_r,
                r_bot, r_top, r_right, r_left, r_br, r_bl, r_tr, r_tl, send_sem, recv_sem):
    lon = lax.axis_index("lon")
    lat = lax.axis_index("lat")
    n_lon = lax.axis_size("lon")
    n_lat = lax.axis_size("lat")
    west = lax.rem(lon + n_lon - 1, n_lon)
    east = lax.rem(lon + 1, n_lon)
    north = lax.rem(lat + n_lat - 1, n_lat)
    south = lax.rem(lat + 1, n_lat)
    barrier = pltpu.get_barrier_semaphore()
    places = ((lon, north), (lon, south), (west, lat), (east, lat),
              (west, north), (east, north), (west, south), (east, south))
    for place in places:
        pl.semaphore_signal(barrier, inc=1, device_id=place, device_id_type=MESH)

    xf[...] = x_ref[...].astype(F32).reshape(64 * 64, 128)
    ii = lax.broadcasted_iota(jnp.int32, (128, 128), 0)
    jj = lax.broadcasted_iota(jnp.int32, (128, 128), 1)
    eye = (ii == jj).astype(BF)

    def turn(k):
        rows = jnp.concatenate(
            [xf[pl.ds(2 * k, 64, 64), :], xf[pl.ds(2 * k + 1, 64, 64), :]], axis=0
        ).astype(BF)
        cells = lax.dot_general(eye, rows, NEG, preferred_element_type=F32)
        fx[k + 2, 4:132, :] = cells
        colf[0, pl.ds(pl.multiple_of(4 * k, 4), 4), :] = cells[0:4]
        colf[1, pl.ds(pl.multiple_of(4 * k, 4), 4), :] = cells[124:128]

    @pl.loop(0, 32)
    def _(k):
        turn(k)

    row_up[...] = fx[2:4, 4:132, :].astype(BF)
    row_dn[...] = fx[32:34, 4:132, :].astype(BF)
    col_l[...] = colf[0].astype(BF)
    col_r[...] = colf[1].astype(BF)
    pl.semaphore_wait(barrier, 8)
    sends = (
        (row_up, r_bot), (row_dn, r_top), (col_l, r_right), (col_r, r_left),
        (col_l.at[0:16], r_br), (col_r.at[0:16], r_bl),
        (col_l.at[112:128], r_tr), (col_r.at[112:128], r_tl),
    )
    copies = []
    for i, ((src, dst), place) in enumerate(zip(sends, places)):
        copies.append(pltpu.make_async_remote_copy(
            src_ref=src, dst_ref=dst, send_sem=send_sem.at[i], recv_sem=recv_sem.at[i],
            device_id=place, device_id_type=MESH,
        ))
        copies[-1].start()
    for copy in copies:
        copy.wait()

    fx[0:2, 4:132, :] = r_top[...].astype(F32)
    fx[34:36, 4:132, :] = r_bot[...].astype(F32)
    colf[0] = r_left[...].astype(F32)
    colf[1] = r_right[...].astype(F32)

    @pl.loop(0, 32)
    def _(k):
        fx[k + 2, 0:4, :] = colf[0, pl.ds(pl.multiple_of(4 * k, 4), 4), :]
        fx[k + 2, 132:136, :] = colf[1, pl.ds(pl.multiple_of(4 * k, 4), 4), :]

    tl = r_tl[...].astype(F32)
    tr = r_tr[...].astype(F32)
    bl = r_bl[...].astype(F32)
    br = r_br[...].astype(F32)
    for h in range(2):
        fx[h, 0:4, :] = tl[8 + 4 * h:12 + 4 * h]
        fx[h, 132:136, :] = tr[8 + 4 * h:12 + 4 * h]
        fx[34 + h, 0:4, :] = bl[4 * h:4 * h + 4]
        fx[34 + h, 132:136, :] = br[4 * h:4 * h + 4]

    @pl.when(lat == 0)
    def _():
        fx[0:2, :, :] = jnp.zeros((2, PITCH, 128), F32)

    @pl.when(lat == n_lat - 1)
    def _():
        fx[34:36, :, :] = jnp.zeros((2, PITCH, 128), F32)

    @pl.loop(0, 36)
    def _(k):
        for q in range(Q):
            p_ref[k, q] = fx[k, pl.ds(q, S, W), :].astype(BF)


def exchange(x):
    scratch = [
        pltpu.VMEM((64 * 64, 128), F32),
        pltpu.VMEM((36, PITCH, 128), F32),
        pltpu.VMEM((2, 128, 128), BF),
        pltpu.VMEM((2, 128, 128), BF),
        pltpu.VMEM((2, 128, 128), F32),
        pltpu.VMEM((128, 128), BF),
        pltpu.VMEM((128, 128), BF),
        pltpu.VMEM((2, 128, 128), BF),
        pltpu.VMEM((2, 128, 128), BF),
        pltpu.VMEM((128, 128), BF),
        pltpu.VMEM((128, 128), BF),
        pltpu.VMEM((16, 128), BF),
        pltpu.VMEM((16, 128), BF),
        pltpu.VMEM((16, 128), BF),
        pltpu.VMEM((16, 128), BF),
        pltpu.SemaphoreType.DMA((8,)),
        pltpu.SemaphoreType.DMA((8,)),
    ]
    return pl.pallas_call(
        halo_kernel,
        out_shape=jax.ShapeDtypeStruct((36, Q, S, 128), BF),
        in_specs=[pl.BlockSpec(memory_space=pltpu.VMEM)],
        out_specs=pl.BlockSpec(memory_space=pltpu.VMEM),
        scratch_shapes=scratch,
        compiler_params=pltpu.CompilerParams(
            collective_id=0, has_side_effects=True, vmem_limit_bytes=24 * 2**20
        ),
        name="halo",
    )(x)


def silu(v):
    half = 0.5 * v
    return half + half * jnp.tanh(half)


def gelu(v):
    inner = 0.7978845608028654 * (v + 0.044715 * (v * v * v))
    half = 0.5 * v
    return half + half * jnp.tanh(inner)


def norm(v):
    centred = v - jnp.mean(v, axis=-1, keepdims=True)
    return centred * lax.rsqrt(jnp.mean(centred * centred, axis=-1, keepdims=True) + 1e-05)


def main_kernel(p_ref, first_ref, rest_ref, patch_ref, count_ref, pos_ref, mix_ref, head_ref,
                embed_hbm, up_hbm, down_hbm, feat_hbm, score_ref,
                wt1, wts, xa, xb, f4, fo, tok, embed_v, up_v, down_v, tokens_v, normed_v,
                hidden_v, pooled_v, sc_v, wsem, fsem):
    lat = lax.axis_index("lat")
    n_lat = lax.axis_size("lat")
    loads = [
        pltpu.make_async_copy(embed_hbm, embed_v, wsem.at[0]),
        pltpu.make_async_copy(up_hbm, up_v, wsem.at[1]),
        pltpu.make_async_copy(down_hbm, down_v, wsem.at[2]),
    ]
    for load in loads:
        load.start()

    for ro in range(2):
        for p in range(2):
            for dq in range(3):
                blocks = []
                for half in range(2):
                    a = 2 * p + half - ro
                    blocks.append(first_ref[a * 3 + dq] if 0 <= a < 3 else jnp.zeros((128, 64), BF))
                    at = ((p * 3 + dq) * 2 + half) * 128
                    for l in range(3):
                        wts[l, ro * 128:ro * 128 + 128, at:at + 128] = (
                            rest_ref[l * 9 + a * 3 + dq] if 0 <= a < 3 else jnp.zeros((128, 128), BF)
                        )
                at = (p * 3 + dq) * 128
                wt1[ro * 128:ro * 128 + 128, at:at + 128] = jnp.concatenate(blocks, axis=1)

    def window(src, k, r):
        slabs = []
        for p in range(2):
            for dq in range(3):
                part = src[pl.ds(k + p, r), dq:dq + W]
                slabs.append(part.reshape(r * COLS, part.shape[-1]))
        return jnp.concatenate(slabs, axis=1)

    def conv(src, k, r, weights):
        summed = lax.dot_general(window(src, k, r), weights, NEG, preferred_element_type=F32)
        return silu(summed).reshape(r, W, S, 256)

    def layer(src, dst, weights, pairs, r):
        def chunk(k, n):
            y = conv(src, k, n, weights[...])
            dst[pl.ds(k, n), 0:W] = y.astype(BF)
            for e in range(2):
                for i in range(n):
                    dst[k + i, W + e] = pltpu.roll(y[i, e], S - 1, 0).astype(BF)

        @pl.loop(0, pairs // r)
        def _(step):
            chunk(step * r, r)

        if pairs % r:
            chunk(pairs - pairs % r, pairs % r)

    def blank(dst, pair, lo, hi):
        dst[pair, :, :, lo:hi] = jnp.zeros((Q, S, hi - lo), BF)

    layer(p_ref, xa, wt1, 35, 5)

    @pl.when(lat == 0)
    def _():
        blank(xa, 0, 0, 256)
        blank(xa, 1, 0, 128)

    @pl.when(lat == n_lat - 1)
    def _():
        blank(xa, 33, 128, 256)
        blank(xa, 34, 0, 256)

    layer(xa, xb, wts.at[0], 34, 4)

    @pl.when(lat == 0)
    def _():
        blank(xb, 0, 0, 256)

    @pl.when(lat == n_lat - 1)
    def _():
        blank(xb, 33, 0, 256)

    layer(xb, xa, wts.at[1], 33, 4)

    @pl.when(lat == 0)
    def _():
        blank(xa, 0, 0, 128)

    @pl.when(lat == n_lat - 1)
    def _():
        blank(xa, 32, 128, 256)

    def feat_copy(step):
        return pltpu.make_async_copy(
            fo.at[pl.ds(step * 8, 8)], feat_hbm.at[pl.ds(step * 8, 8)], fsem
        )

    @pl.loop(0, 8)
    def _(step):
        y = conv(xa, step * 4, 4, wts[2])
        for i in range(4):
            for half in range(2):
                for q in range(W):
                    f4[i * 2 + half, pl.ds(q, S, W), :] = y[i, q, :, half * 128:half * 128 + 128]
        for row in range(8):
            fo[step * 8 + row] = f4[row, 0:128, :].astype(BF)
        feat_copy(step).start()
        for ar in range(2):
            for b2 in range(2):
                at = pl.multiple_of(step * 64 + ar * 32 + b2 * 16, 16)
                for u in range(4):
                    for v in range(4):
                        two = [f4[ar * 4 + u, pl.ds(4 * (2 * b2 + b) + v, 8, 16), :] for b in range(2)]
                        lane = (u * 4 + v) * 128
                        tok[pl.ds(at, 16), lane:lane + 128] = jnp.concatenate(two, axis=0).astype(BF)

    loads[0].wait()

    @pl.loop(0, 4)
    def _(n):
        lanes = pl.ds(pl.multiple_of(n * 256, 256), 256)
        summed = jnp.dot(tok[...], embed_v[:, lanes], preferred_element_type=F32)
        place = pos_ref[:, lanes].astype(F32)
        wide = summed.reshape(4, 16, 8, 256) + place[None, :, None, :]
        tokens_v[:, lanes] = wide.reshape(512, 256).astype(BF)

    ti = lax.broadcasted_iota(jnp.int32, (128, 16), 0) // 8
    tj = lax.broadcasted_iota(jnp.int32, (128, 16), 1)
    pick = (ti == tj).astype(BF)
    spread = jnp.dot(pick, mix_ref[...], preferred_element_type=F32).astype(BF)
    spread = lax.dot_general(spread, pick, NEG, preferred_element_type=F32)
    ri = lax.broadcasted_iota(jnp.int32, (128, 128), 0) % 8
    rj = lax.broadcasted_iota(jnp.int32, (128, 128), 1) % 8
    mix = jnp.where(ri == rj, spread, 0.0).astype(BF)

    @pl.loop(0, 4)
    def _(pi):
        rows = pl.ds(pl.multiple_of(pi * 128, 128), 128)
        wide = tokens_v[rows, :].astype(F32)
        mixing = jnp.dot(mix, norm(wide).astype(BF), preferred_element_type=F32)
        mixed = (wide + mixing).astype(BF)
        tokens_v[rows, :] = mixed
        normed_v[rows, :] = norm(mixed.astype(F32)).astype(BF)

    loads[1].wait()

    @pl.loop(0, 16)
    def _(n):
        lanes = pl.ds(pl.multiple_of(n * 256, 256), 256)
        hidden = jnp.dot(normed_v[...], up_v[:, lanes], preferred_element_type=F32)
        hidden_v[:, lanes] = gelu(hidden).astype(BF)

    loads[2].wait()

    @pl.loop(0, 4)
    def _(pi):
        rows = pl.ds(pl.multiple_of(pi * 128, 128), 128)
        summed = jnp.dot(hidden_v[rows, :], down_v[...], preferred_element_type=F32)
        encoded = norm(tokens_v[rows, :].astype(F32) + summed)
        total = jnp.sum(encoded.reshape(16, 8, 1024), axis=0)
        pooled_v[pl.ds(pl.multiple_of(pi * 8, 8), 8), :] = total * 0.0625

    sc_v[...] = jnp.dot(pooled_v[...].astype(BF), head_ref[...], preferred_element_type=F32)
    for s in range(32):
        line = sc_v[pl.ds(patch_ref[s], 1), :]
        score_ref[pl.ds(s, 1), :] = jnp.where(s < count_ref[0], line, 0.0)

    pltpu.make_async_copy(fo, feat_hbm, fsem).wait()


def classify(p, first, rest, patch, count, pos, mix, head, embed, up, down):
    vm = pl.BlockSpec(memory_space=pltpu.VMEM)
    sm = pl.BlockSpec(memory_space=pltpu.SMEM)
    hb = pl.BlockSpec(memory_space=pl.ANY)
    return pl.pallas_call(
        main_kernel,
        out_shape=(
            jax.ShapeDtypeStruct((64, 128, 128), BF),
            jax.ShapeDtypeStruct((32, 8), F32),
        ),
        in_specs=[vm, vm, vm, sm, sm, vm, vm, vm, hb, hb, hb],
        out_specs=(hb, vm),
        scratch_shapes=[
            pltpu.VMEM((256, 768), BF),
            pltpu.VMEM((3, 256, 1536), BF),
            pltpu.VMEM((35, Q, S, 256), BF),
            pltpu.VMEM((34, Q, S, 256), BF),
            pltpu.VMEM((8, COLS, 128), F32),
            pltpu.VMEM((64, 128, 128), BF),
            pltpu.VMEM((512, 2048), BF),
            pltpu.VMEM((2048, 1024), BF),
            pltpu.VMEM((1024, 4096), BF),
            pltpu.VMEM((4096, 1024), BF),
            pltpu.VMEM((512, 1024), BF),
            pltpu.VMEM((512, 1024), BF),
            pltpu.VMEM((512, 4096), BF),
            pltpu.VMEM((32, 1024), F32),
            pltpu.VMEM((32, 8), F32),
            pltpu.SemaphoreType.DMA((3,)),
            pltpu.SemaphoreType.DMA,
        ],
        compiler_params=pltpu.CompilerParams(vmem_limit_bytes=60 * 2**20),
        name="classify",
    )(p, first, rest, patch, count, pos, mix, head, embed, up, down)


def on_device(input_field, conv_first, conv_rest, flag_patch, flag_count, w_embed, pos_embed,
              token_mix, w_up, w_down, w_head):
    p = exchange(input_field)
    features, scores = classify(
        p, conv_first.reshape(9, 128, 64), conv_rest.reshape(27, 128, 128),
        flag_patch.reshape(32), flag_count.reshape(1), pos_embed, token_mix, w_head,
        w_embed, w_up, w_down,
    )
    return (features, scores[None, None])


def solution(mesh):
    placed = (
        P(None, "lat", "lon"), P(), P(), P("lat", "lon", None), P("lat", "lon"),
        P(), P(), P(), P(), P(), P(),
    )
    return jax.shard_map(
        on_device,
        mesh=mesh,
        in_specs=placed,
        out_specs=(P("lat", "lon", None), P("lat", "lon", None, None)),
        check_vma=False,
    )
```

```python
import functools

import jax
import jax.numpy as jnp
from jax import lax
from jax.experimental import pallas as pl
from jax.experimental.pallas import tpu as pltpu
from jax.sharding import PartitionSpec as P

BF = jnp.bfloat16
F32 = jnp.float32
MESH = pl.DeviceIdType.MESH

W = 8
Q = W + 2
S = 16
COLS = W * S
STRIP = 48
HELD = 56
NEG = (((1,), (1,)), ((), ()))
POS = (((1,), (0,)), ((), ()))


def silu(v):
    half = 0.5 * v
    return half + half * jnp.tanh(half)


def gelu(v):
    v = v.astype(BF)
    half = BF(0.5) * v
    return half + half * jnp.tanh(v * (BF(0.7978845608028654) + BF(0.035677408136300125) * (v * v)))


def norm(v):
    centred = v - jnp.mean(v, axis=-1, keepdims=True)
    return centred * lax.rsqrt(jnp.mean(centred * centred, axis=-1, keepdims=True) + 1e-05)


def conv_kernel(x_hbm, first_hbm, rest_hbm, embed_hbm, fo, tok, embed_v, x_ref, first_ref, rest_ref, xf, x0, x1, x2, x3, f4, wt1, wts,
                colf, col_l, col_r, sf0, sf1, sf2, sf3, r_right, r_left, r_br, r_bl, r_tr, r_tl,
                send_sem, recv_sem, load_sem):
    loads = [
        pltpu.make_async_copy(x_hbm, x_ref, load_sem.at[0]),
        pltpu.make_async_copy(first_hbm, first_ref, load_sem.at[1]),
        pltpu.make_async_copy(rest_hbm, rest_ref, load_sem.at[2]),
        pltpu.make_async_copy(embed_hbm, embed_v, load_sem.at[3]),
    ]
    for load in loads:
        load.start()
    lon = lax.axis_index("lon")
    lat = lax.axis_index("lat")
    n_lon = lax.axis_size("lon")
    n_lat = lax.axis_size("lat")
    west = lax.rem(lon + n_lon - 1, n_lon)
    east = lax.rem(lon + 1, n_lon)
    north = lax.rem(lat + n_lat - 1, n_lat)
    south = lax.rem(lat + 1, n_lat)
    barrier = pltpu.get_barrier_semaphore()
    places = ((lon, north), (lon, south), (west, lat), (east, lat),
              (west, north), (east, north), (west, south), (east, south))
    for place in places:
        pl.semaphore_signal(barrier, inc=1, device_id=place, device_id_type=MESH)
    low = jnp.where(lat == 0, 0, -64)
    high = jnp.where(lat == n_lat - 1, 64, 128)

    loads[0].wait()
    xf[...] = x_ref[...].astype(F32).reshape(64 * 64, 128)
    mm = lax.broadcasted_iota(jnp.int32, (Q * S, 128), 0)
    jj = lax.broadcasted_iota(jnp.int32, (Q * S, 128), 1)
    order = (jj == mm % S * W + mm // S - 1).astype(BF)

    def turn(k):
        rows = jnp.concatenate(
            [xf[pl.ds(2 * k + i, 64, 64), :] for i in range(4)], axis=0
        ).astype(BF)
        cells = lax.dot_general(order, rows, NEG, preferred_element_type=F32)
        for h in range(2):
            own = cells[:, h * 128:h * 128 + 128].reshape(Q, S, 128)
            x0[k + 2 + h] = own.astype(BF)
            for c in range(4):
                colf[0, c, pl.ds(k + h, 1), :] = own[c + 1, 0:1]
                colf[1, c, pl.ds(k + h, 1), :] = own[c + 5, 15:16]
            for c in range(2):
                sf0[0, 4 + c, pl.ds(k + 2 + h, 1), :] = own[c + 1, 0:1]
                sf0[1, c, pl.ds(k + 2 + h, 1), :] = own[c + 7, 15:16]

    @pl.loop(0, 16, unroll=2)
    def _(k):
        turn(2 * k)

    col_l[...] = colf[0].astype(BF)
    col_r[...] = colf[1].astype(BF)

    loads[1].wait()
    loads[2].wait()
    for ro in range(2):
        out = slice(ro * 128, ro * 128 + 128)
        for p in range(2):
            for dq in range(3):
                for half in range(2):
                    a = 2 * p + half - ro
                    at = (p * 3 + dq) * 2 + half
                    wt1[at * 64:at * 64 + 64, out] = (
                        first_ref[a * 3 + dq] if 0 <= a < 3 else jnp.zeros((64, 128), BF)
                    )
                    for l in range(3):
                        wts[l, out, at * 128:at * 128 + 128] = (
                            rest_ref[l * 9 + a * 3 + dq] if 0 <= a < 3 else jnp.zeros((128, 128), BF)
                        )

    xs = (x0, x1, x2, x3)
    sfs = (sf0, sf1, sf2, sf3)

    def taps(l):
        return (wt1[...], POS) if l == 1 else (wts[l - 2], NEG)

    def rows_of(src, k, r):
        slabs = []
        for p in range(2):
            for dq in range(3):
                part = src[pl.ds(k + p, r), dq:dq + W]
                slabs.append(part.reshape(r * COLS, part.shape[-1]))
        return jnp.concatenate(slabs, axis=1)

    def keep(l, k, y, border):
        n = y.shape[0]
        if border and l < 4:
            pair = lax.broadcasted_iota(jnp.int32, (n, 1, 1, 256), 0)
            lane = lax.broadcasted_iota(jnp.int32, (n, 1, 1, 256), 3)
            row = l - 4 + 2 * (k + pair) + lane // 128
            y = jnp.where((row >= low) & (row < high), y, 0.0)
        if l == 4:
            for i in range(n):
                for half in range(2):
                    for q in range(W):
                        f4[pl.ds((2 * (k + i) + half) * COLS + q, S, W), :] = (
                            y[i, q, :, half * 128:half * 128 + 128]
                        )
            return
        dst = xs[l]
        dst[pl.ds(k, n), 1:W + 1] = y.astype(BF)
        sf = sfs[l]
        for i in range(n):
            dst[k + i, 0] = pltpu.roll(y[i, W - 1], 1, 0).astype(BF)
            dst[k + i, W + 1] = pltpu.roll(y[i, 0], S - 1, 0).astype(BF)
            for c in range(2):
                sf[0, 4 + c, pl.ds(k + i, 1), :] = y[i, l + c, 0:1]
                sf[1, c, pl.ds(k + i, 1), :] = y[i, W - 2 - l + c, S - 1:S]

    def main(l, k, r, border=False):
        weights, dims = taps(l)
        summed = lax.dot_general(rows_of(xs[l - 1], k, r), weights, dims, preferred_element_type=F32)
        keep(l, k, silu(summed).reshape(r, W, S, 256), border)

    def inner(l, r, first=0, last=None):
        pairs = 32 - l
        steps = (pairs + r - 1) // r

        @pl.loop(first, steps if last is None else last)
        def _(step):
            main(l, jnp.minimum(2 + step * r, 2 + pairs - r), r)

    inner(1, 8)
    inner(2, 10, 0, 1)

    pl.semaphore_wait(barrier, 8)
    sends = (
        (x0.at[2:4], x0.at[34:36]), (x0.at[32:34], x0.at[0:2]), (col_l, r_right), (col_r, r_left),
        (col_l.at[:, 0:16], r_br), (col_r.at[:, 0:16], r_bl),
        (col_l.at[:, 16:32], r_tr), (col_r.at[:, 16:32], r_tl),
    )
    copies = []
    for i, ((src, dst), place) in enumerate(zip(sends, places)):
        copies.append(pltpu.make_async_remote_copy(
            src_ref=src, dst_ref=dst, send_sem=send_sem.at[i], recv_sem=recv_sem.at[i],
            device_id=place, device_id_type=MESH,
        ))
        copies[-1].start()

    inner(2, 10, 1)
    inner(3, 10)
    inner(4, 7)

    loads[3].wait()
    for copy in copies:
        copy.wait()

    @pl.when(lat == 0)
    def _():
        x0[0:2] = jnp.zeros((2, Q, S, 128), BF)

    @pl.when(lat == n_lat - 1)
    def _():
        x0[34:36] = jnp.zeros((2, Q, S, 128), BF)

    sf0[0, 0:4, 2:34, :] = r_left[...].astype(F32)
    sf0[1, 2:6, 2:34, :] = r_right[...].astype(F32)
    sf0[0, 0:4, 0:2, :] = r_tl[...].astype(F32)[:, 14:16]
    sf0[1, 2:6, 0:2, :] = r_tr[...].astype(F32)[:, 14:16]
    sf0[0, 0:4, 34:36, :] = r_bl[...].astype(F32)[:, 0:2]
    sf0[1, 2:6, 34:36, :] = r_br[...].astype(F32)[:, 0:2]
    for k in (0, 1, 34, 35):
        for c in range(2):
            sf0[0, 4 + c, k:k + 1, :] = x0[k, c + 1].astype(F32)[0:1]
            sf0[1, c, k:k + 1, :] = x0[k, c + 7].astype(F32)[15:16]

    @pl.when(lat == 0)
    def _():
        sf0[:, :, 0:2, :] = jnp.zeros((2, 6, 2, 128), F32)

    @pl.when(lat == n_lat - 1)
    def _():
        sf0[:, :, 34:36, :] = jnp.zeros((2, 6, 2, 128), F32)

    def strips(l):
        src = sfs[l - 1]
        wide = src.shape[-1]
        weights, dims = taps(l)
        slabs = []
        for p in range(2):
            for dq in range(3):
                part = src[:, dq:dq + 4, p:p + STRIP, :].astype(BF)
                slabs.append(part.reshape(8 * STRIP, wide))
        summed = lax.dot_general(jnp.concatenate(slabs, axis=1), weights, dims,
                                 preferred_element_type=F32)
        y = silu(summed).reshape(2, 4, STRIP, 256)
        if l == 4:
            for side in range(2):
                for c in range(4):
                    for half in range(2):
                        f4[pl.ds(half * COLS + 124 * side + c, 32, 2 * COLS), :] = (
                            y[side, c, 0:32, half * 128:half * 128 + 128]
                        )
            return
        pair = lax.broadcasted_iota(jnp.int32, (1, 1, STRIP, 256), 2)
        lane = lax.broadcasted_iota(jnp.int32, (1, 1, STRIP, 256), 3)
        row = l - 4 + 2 * pair + lane // 128
        y = jnp.where((row >= low) & (row < high), y, 0.0)
        sfs[l][0, 0:4, 0:STRIP, :] = y[0]
        sfs[l][1, 2:6, 0:STRIP, :] = y[1]

    for l in range(1, 5):
        main(l, 0, 2, True)
        main(l, 34 - l, 2, True)
        strips(l)

    @pl.loop(0, 16)
    def _(tr):
        for u in range(4):
            row = pl.multiple_of((tr * 4 + u) * COLS, COLS)
            fo[tr * 4 + u] = f4[pl.ds(row, COLS), :].astype(BF)
            for b2 in range(2):
                at = pl.multiple_of(tr * 32 + b2 * 16, 16)
                for v in range(4):
                    two = [f4[pl.ds(row + 4 * (2 * b2 + b) + v, 8, 16), :] for b in range(2)]
                    lane = (u * 4 + v) * 128
                    tok[pl.ds(at, 16), lane:lane + 128] = jnp.concatenate(two, axis=0).astype(BF)


def convolve(x, first, rest, embed):
    vm = pl.BlockSpec(memory_space=pltpu.VMEM)
    hb = pl.BlockSpec(memory_space=pltpu.HBM)
    side = pltpu.VMEM((4, 32, 128), BF)
    corner = pltpu.VMEM((4, 16, 128), BF)
    return pl.pallas_call(
        conv_kernel,
        out_shape=(
            jax.ShapeDtypeStruct((64, 128, 128), BF),
            jax.ShapeDtypeStruct((512, 2048), BF),
            jax.ShapeDtypeStruct((2048, 1024), BF),
        ),
        in_specs=[hb, hb, hb, hb],
        out_specs=(vm, vm, vm),
        scratch_shapes=[
            pltpu.VMEM((64, 64, 128), BF),
            pltpu.VMEM((9, 64, 128), BF),
            pltpu.VMEM((27, 128, 128), BF),
            pltpu.VMEM((64 * 64, 128), F32),
            pltpu.VMEM((36, Q, S, 128), BF),
            pltpu.VMEM((35, Q, S, 256), BF),
            pltpu.VMEM((34, Q, S, 256), BF),
            pltpu.VMEM((33, Q, S, 256), BF),
            pltpu.VMEM((64 * 128, 128), F32),
            pltpu.VMEM((768, 256), BF),
            pltpu.VMEM((3, 256, 1536), BF),
            pltpu.VMEM((2, 4, 32, 128), F32),
            side, side,
            pltpu.VMEM((2, 6, HELD, 128), F32),
            pltpu.VMEM((2, 6, HELD, 256), F32),
            pltpu.VMEM((2, 6, HELD, 256), F32),
            pltpu.VMEM((2, 6, HELD, 256), F32),
            side, side, corner, corner, corner, corner,
            pltpu.SemaphoreType.DMA((8,)),
            pltpu.SemaphoreType.DMA((8,)),
            pltpu.SemaphoreType.DMA((4,)),
        ],
        compiler_params=pltpu.CompilerParams(
            collective_id=0, has_side_effects=True, vmem_limit_bytes=36 * 2**20
        ),
        name="convolve",
    )(*in_hbm(x, first, rest, embed))


def token_kernel(tok, fo, embed_v, count_ref, patch_hbm, pos_hbm, mix_hbm, head_hbm, up_hbm, down_hbm,
                 feat_hbm, score_ref, patch_ref, pos_ref, mix_ref, head_ref,
                 up_v, down_v, tokens_v, normed_v, hidden_v, pooled_v, sc_v, wsem, fsem):
    pairs = (
        (pos_hbm, pos_ref), (up_hbm, up_v), (down_hbm, down_v), (mix_hbm, mix_ref),
        (head_hbm, head_ref), (patch_hbm, patch_ref),
    )
    loads = [pltpu.make_async_copy(src, dst, wsem.at[i]) for i, (src, dst) in enumerate(pairs)]
    for i in (0, 3, 4, 5, 1, 2):
        loads[i].start()
    feat_copy = pltpu.make_async_copy(fo, feat_hbm, fsem)
    feat_copy.start()

    loads[0].wait()

    @pl.loop(0, 2)
    def _(n):
        lanes = pl.ds(pl.multiple_of(n * 512, 512), 512)
        summed = jnp.dot(tok[...], embed_v[:, lanes], preferred_element_type=F32)
        place = pos_ref[:, lanes].astype(F32)
        wide = summed.reshape(4, 16, 8, 512) + place[None, :, None, :]
        tokens_v[:, lanes] = wide.reshape(512, 512).astype(BF)

    loads[3].wait()
    ti = lax.broadcasted_iota(jnp.int32, (128, 16), 0) // 8
    tj = lax.broadcasted_iota(jnp.int32, (128, 16), 1)
    pick = (ti == tj).astype(BF)
    spread = jnp.dot(pick, mix_ref[...], preferred_element_type=F32).astype(BF)
    spread = lax.dot_general(spread, pick, NEG, preferred_element_type=F32)
    ri = lax.broadcasted_iota(jnp.int32, (128, 128), 0) % 8
    rj = lax.broadcasted_iota(jnp.int32, (128, 128), 1) % 8
    mix = jnp.where(ri == rj, spread, 0.0).astype(BF)

    @pl.loop(0, 4, unroll=2)
    def _(pi):
        rows = pl.ds(pl.multiple_of(pi * 128, 128), 128)
        wide = tokens_v[rows, :].astype(F32)
        mixing = jnp.dot(mix, norm(wide).astype(BF), preferred_element_type=F32)
        mixed = (wide + mixing).astype(BF)
        tokens_v[rows, :] = mixed
        normed_v[rows, :] = norm(mixed.astype(F32)).astype(BF)

    loads[1].wait()

    @pl.loop(0, 4)
    def _(n):
        lanes = pl.ds(pl.multiple_of(n * 1024, 1024), 1024)
        hidden = jnp.dot(normed_v[...], up_v[:, lanes], preferred_element_type=F32)
        hidden_v[:, lanes] = gelu(hidden)

    loads[2].wait()

    @pl.loop(0, 2)
    def _(pi):
        rows = pl.ds(pl.multiple_of(pi * 256, 256), 256)
        summed = jnp.dot(hidden_v[rows, :], down_v[...], preferred_element_type=F32)
        encoded = norm(tokens_v[rows, :].astype(F32) + summed)
        total = jnp.sum(encoded.reshape(2, 16, 8, 1024), axis=1)
        pooled_v[pl.ds(pl.multiple_of(pi * 16, 16), 16), :] = total.reshape(16, 1024) * 0.0625

    for load in loads[4:]:
        load.wait()
    sc_v[0, :, 0:8] = lax.dot_general(
        pooled_v[...].astype(BF), head_ref[...], NEG, preferred_element_type=F32
    )
    for s in range(32):
        line = sc_v[0, pl.ds(patch_ref[0, 0, s], 1), :]
        sc_v[1, pl.ds(s, 1), :] = jnp.where(s < count_ref[0, 0], line, 0.0)
    score_ref[...] = jnp.transpose(sc_v[1], (1, 0))[0:8]
    feat_copy.wait()


def classify(tok, fo, embed, patch, count, pos, mix, head, up, down):
    vm = pl.BlockSpec(memory_space=pltpu.VMEM)
    hb = pl.BlockSpec(memory_space=pltpu.HBM)
    return pl.pallas_call(
        token_kernel,
        out_shape=(
            jax.ShapeDtypeStruct((64, 128, 128), BF),
            jax.ShapeDtypeStruct((8, 32), F32),
        ),
        in_specs=[vm, vm, vm, pl.BlockSpec(memory_space=pltpu.SMEM)] + [hb] * 6,
        out_specs=(hb, vm),
        scratch_shapes=[
            pltpu.SMEM((1, 1, 32), jnp.int32),
            pltpu.VMEM((16, 1024), BF),
            pltpu.VMEM((16, 16), BF),
            pltpu.VMEM((8, 1024), BF),
            pltpu.VMEM((1024, 4096), BF),
            pltpu.VMEM((4096, 1024), BF),
            pltpu.VMEM((512, 1024), BF),
            pltpu.VMEM((512, 1024), BF),
            pltpu.VMEM((512, 4096), BF),
            pltpu.VMEM((32, 1024), F32),
            pltpu.VMEM((2, 32, 128), F32),
            pltpu.SemaphoreType.DMA((6,)),
            pltpu.SemaphoreType.DMA,
        ],
        compiler_params=pltpu.CompilerParams(vmem_limit_bytes=40 * 2**20),
        name="classify",
    )(tok, fo, embed, count, *in_hbm(patch, pos, mix, head, up, down))


def in_hbm(*arrays):
    return tuple(pltpu.with_memory_space_constraint(a, pltpu.HBM) for a in arrays)


def on_device(input_field, conv_first, conv_rest, flag_patch, flag_count, w_embed, pos_embed,
              token_mix, w_up, w_down, w_head):
    fo, tok, embed = convolve(
        input_field, jnp.transpose(conv_first, (0, 1, 3, 2)).reshape(9, 64, 128),
        conv_rest.reshape(27, 128, 128), w_embed,
    )
    features, scores = classify(
        tok, fo, embed, flag_patch, flag_count, pos_embed, token_mix, w_head.T, w_up, w_down,
    )
    return (features, scores.T[None, None])


def solution(mesh):
    placed = (
        P(None, "lat", "lon"), P(), P(), P("lat", "lon", None), P("lat", "lon"),
        P(), P(), P(), P(), P(), P(),
    )
    return jax.shard_map(
        on_device,
        mesh=mesh,
        in_specs=placed,
        out_specs=(P("lat", "lon", None), P("lat", "lon", None, None)),
        check_vma=False,
    )
```

```python
import functools

import jax
import jax.numpy as jnp
from jax import lax
from jax.experimental import pallas as pl
from jax.experimental.pallas import tpu as pltpu
from jax.sharding import PartitionSpec as P

BF = jnp.bfloat16
F32 = jnp.float32
MESH = pl.DeviceIdType.MESH

W = 8
Q = W + 2
S = 16
COLS = W * S
STRIP = 40
HELD = 48
NEG = (((1,), (1,)), ((), ()))
POS = (((1,), (0,)), ((), ()))


def silu(v):
    half = 0.5 * v
    return half + half * jnp.tanh(half)


def gelu(v):
    v = v.astype(BF)
    half = BF(0.5) * v
    return half + half * jnp.tanh(v * (BF(0.7978845608028654) + BF(0.035677408136300125) * (v * v)))


def norm(v):
    centred = v - jnp.mean(v, axis=-1, keepdims=True)
    return centred * lax.rsqrt(jnp.mean(centred * centred, axis=-1, keepdims=True) + 1e-05)


def conv_kernel(x_hbm, first_hbm, rest_hbm, embed_hbm, fo, tok, embed_v, x_ref, first_ref, rest_ref, xf, x0, x1, x2, x3, f4, wt1, wm, we,
                colf, cornf, corner, col_l, col_r, sf0, sf1, sf2, sf3, r_right, r_left, r_br, r_bl, r_tr, r_tl,
                send_sem, recv_sem, load_sem):
    loads = [
        pltpu.make_async_copy(x_hbm, x_ref, load_sem.at[0]),
        pltpu.make_async_copy(first_hbm, first_ref, load_sem.at[1]),
        pltpu.make_async_copy(rest_hbm, rest_ref, load_sem.at[2]),
        pltpu.make_async_copy(embed_hbm, embed_v, load_sem.at[3]),
    ]
    for load in loads:
        load.start()
    lon = lax.axis_index("lon")
    lat = lax.axis_index("lat")
    n_lon = lax.axis_size("lon")
    n_lat = lax.axis_size("lat")
    west = lax.rem(lon + n_lon - 1, n_lon)
    east = lax.rem(lon + 1, n_lon)
    north = lax.rem(lat + n_lat - 1, n_lat)
    south = lax.rem(lat + 1, n_lat)
    barrier = pltpu.get_barrier_semaphore()
    places = ((lon, north), (lon, south), (west, lat), (east, lat),
              (west, north), (east, north), (west, south), (east, south))
    for place in places:
        pl.semaphore_signal(barrier, inc=1, device_id=place, device_id_type=MESH)
    low = jnp.where(lat == 0, 0, -64)
    high = jnp.where(lat == n_lat - 1, 64, 128)

    loads[0].wait()
    xf[...] = x_ref[...].astype(F32).reshape(64 * 64, 128)
    mm = lax.broadcasted_iota(jnp.int32, (Q * S, 128), 0)
    jj = lax.broadcasted_iota(jnp.int32, (Q * S, 128), 1)
    order = (jj == mm % S * W + mm // S - 1).astype(BF)

    def turn(k):
        rows = jnp.concatenate(
            [xf[pl.ds(2 * k + i, 64, 64), :] for i in range(4)], axis=0
        ).astype(BF)
        cells = lax.dot_general(order, rows, NEG, preferred_element_type=F32)
        for h in range(2):
            own = cells[:, h * 128:h * 128 + 128].reshape(Q, S, 128)
            x0[k + 2 + h] = own.astype(BF)
            for c in range(4):
                colf[0, c, pl.ds(k + h, 1), :] = own[c + 1, 0:1]
                colf[1, c, pl.ds(k + h, 1), :] = own[c + 5, 15:16]
            for c in range(2):
                sf0[0, 4 + c, pl.ds(k + 2 + h, 1), :] = own[c + 1, 0:1]
                sf0[1, c, pl.ds(k + 2 + h, 1), :] = own[c + 7, 15:16]

    @pl.loop(0, 16, unroll=4)
    def _(k):
        turn(2 * k)

    cornf[...] = jnp.zeros((2, 2, 16, 128), F32)
    for e in range(2):
        for end in range(2):
            for c in range(4):
                cornf[e, end, 2 * c:2 * c + 2, :] = colf[e, c, 30 * end:30 * end + 2, :]
    corner[...] = cornf[...].astype(BF)
    col_l[...] = colf[0].astype(BF)
    col_r[...] = colf[1].astype(BF)

    loads[1].wait()
    loads[2].wait()
    for ro in range(2):
        out = slice(ro * 128, ro * 128 + 128)
        for p in range(2):
            for dq in range(3):
                for half in range(2):
                    a = 2 * p + half - ro
                    at = (p * 3 + dq) * 2 + half
                    wt1[at * 64:at * 64 + 64, out] = (
                        first_ref[a * 3 + dq] if 0 <= a < 3 else jnp.zeros((64, 128), BF)
                    )
    for l in range(3):
        for o in range(2):
            out = slice(o * 128, o * 128 + 128)
            for dq in range(3):
                for i in range(2):
                    at = (dq * 2 + i) * 128
                    wm[l, out, at:at + 128] = rest_ref[l * 9 + (i + 1 - o) * 3 + dq]
            for e in range(2):
                for t in range(4):
                    b = t - o
                    we[l, e, out, t * 128:t * 128 + 128] = (
                        rest_ref[l * 9 + 6 * e + b] if 0 <= b < 3 else jnp.zeros((128, 128), BF)
                    )

    xs = (x0, x1, x2, x3)
    sfs = (sf0, sf1, sf2, sf3)

    def product(l, groups):
        def stack(p, first, step, *half):
            return jnp.concatenate(
                [get(p, c, *half) for get, n in groups for c in range(first, first + n, step)], axis=0
            )

        def split(whole, parts):
            at = 0
            for size, n in parts:
                yield [whole[at + c * size:at + c * size + size] for c in range(n)]
                at += size * n

        sizes = [(get(0, 0).shape[0], n) for get, n in groups]
        if l == 1:
            slabs = [stack(p, dq, 1) for p in range(2) for dq in range(3)]
            full = jnp.dot(jnp.concatenate(slabs, axis=1), wt1[...], preferred_element_type=F32)
            return list(split(full, sizes))
        slabs = []
        for dq in range(3):
            slabs += [stack(0, dq, 1, 1), stack(1, dq, 1, 0)]
        full = lax.dot_general(jnp.concatenate(slabs, axis=1), wm[l - 2], NEG, preferred_element_type=F32)
        outer = []
        for e in range(2):
            slabs = [stack(e, t, 2, e) for t in range(4)]
            part = lax.dot_general(
                jnp.concatenate(slabs, axis=1), we[l - 2, e], NEG, preferred_element_type=F32
            )
            outer.append(list(split(part, [(size, n // 2) for size, n in sizes])))
        sums = []
        for g, columns in enumerate(split(full, sizes)):
            for c in range(len(columns)):
                lanes = slice(c % 2 * 128, c % 2 * 128 + 128)
                columns[c] = columns[c] + jnp.concatenate(
                    [part[g][c // 2][:, lanes] for part in outer], axis=1
                )
            sums.append(columns)
        return sums

    def inside(l, first, shape, dim):
        pair = lax.broadcasted_iota(jnp.int32, shape, dim)
        lane = lax.broadcasted_iota(jnp.int32, shape, len(shape) - 1)
        row = l - 4 + 2 * (first + pair) + lane // 128
        return (row >= low) & (row < high)

    def of_main(l, k, r):
        src = xs[l - 1]

        def get(p, c, half=None):
            lanes = slice(None) if half is None else slice(half * 128, half * 128 + 128)
            part = src[pl.ds(k + p, r), c, :, lanes]
            return part.reshape(r * S, part.shape[-1])

        return get, W

    def keep(l, k, r, sums, border=False):
        for q in range(W):
            y = silu(sums[q]).reshape(r, S, 256)
            if border and l < 4:
                y = jnp.where(inside(l, k, (r, S, 256), 0), y, 0.0)
            if l == 4:
                for i in range(r):
                    for half in range(2):
                        f4[pl.ds((2 * (k + i) + half) * COLS + q, S, W), :] = (
                            y[i, :, half * 128:half * 128 + 128]
                        )
                continue
            dst = xs[l]
            dst[pl.ds(k, r), q + 1] = y.astype(BF)
            for i in range(r):
                if q == W - 1:
                    dst[k + i, 0] = pltpu.roll(y[i], 1, 0).astype(BF)
                if q == 0:
                    dst[k + i, W + 1] = pltpu.roll(y[i], S - 1, 0).astype(BF)
                for c in range(2):
                    if q == l + c:
                        sfs[l][0, 4 + c, pl.ds(k + i, 1), :] = y[i, 0:1]
                    if q == W - 2 - l + c:
                        sfs[l][1, c, pl.ds(k + i, 1), :] = y[i, S - 1:S]

    def inner(l, r, first=0, last=None):
        pairs = 32 - l
        steps = (pairs + r - 1) // r

        @pl.loop(first, steps if last is None else last)
        def _(step):
            k = jnp.minimum(2 + step * r, 2 + pairs - r)
            keep(l, k, r, product(l, [of_main(l, k, r)])[0])

    inner(1, 16, 0, 1)

    pl.semaphore_wait(barrier, 8)
    sends = (
        (x0.at[2:4, 1:W + 1], x0.at[34:36, 1:W + 1]), (x0.at[32:34, 1:W + 1], x0.at[0:2, 1:W + 1]),
        (col_l, r_right), (col_r, r_left), (corner.at[0, 0], r_br), (corner.at[1, 0], r_bl),
        (corner.at[0, 1], r_tr), (corner.at[1, 1], r_tl),
    )
    copies = []
    for i, ((src, dst), place) in enumerate(zip(sends, places)):
        copies.append(pltpu.make_async_remote_copy(
            src_ref=src, dst_ref=dst, send_sem=send_sem.at[i], recv_sem=recv_sem.at[i],
            device_id=place, device_id_type=MESH,
        ))
        copies[-1].start()

    inner(1, 16, 1)
    inner(2, 15)
    inner(3, 15)
    inner(4, 14)

    loads[3].wait()
    for copy in copies:
        copy.wait()

    @pl.when(lat == 0)
    def _():
        x0[0:2] = jnp.zeros((2, Q, S, 128), BF)

    @pl.when(lat == n_lat - 1)
    def _():
        x0[34:36] = jnp.zeros((2, Q, S, 128), BF)

    sf0[0, 0:4, 2:34, :] = r_left[...].astype(F32)
    sf0[1, 2:6, 2:34, :] = r_right[...].astype(F32)
    for at, west_end, east_end in ((0, r_tl, r_tr), (34, r_bl, r_br)):
        for e, end in enumerate((west_end, east_end)):
            rows = end[...].astype(F32)
            for c in range(4):
                sf0[e, 2 * e + c, at:at + 2, :] = rows[2 * c:2 * c + 2]
        for k in (at, at + 1):
            first = x0[k, 1].astype(F32)
            last = x0[k, W].astype(F32)
            x0[k, 0] = pltpu.roll(last, 1, 0).astype(BF)
            x0[k, W + 1] = pltpu.roll(first, S - 1, 0).astype(BF)
            sf0[0, 4, k:k + 1, :] = first[0:1]
            sf0[0, 5, k:k + 1, :] = x0[k, 2].astype(F32)[0:1]
            sf0[1, 0, k:k + 1, :] = x0[k, W - 1].astype(F32)[S - 1:S]
            sf0[1, 1, k:k + 1, :] = last[S - 1:S]

    @pl.when(lat == 0)
    def _():
        sf0[:, :, 0:2, :] = jnp.zeros((2, 6, 2, 128), F32)

    @pl.when(lat == n_lat - 1)
    def _():
        sf0[:, :, 34:36, :] = jnp.zeros((2, 6, 2, 128), F32)

    def of_strips(l):
        src = sfs[l - 1]

        def get(p, c, half=None):
            lanes = slice(None) if half is None else slice(half * 128, half * 128 + 128)
            part = src[:, c, p:p + STRIP, lanes]
            return part.reshape(2 * STRIP, part.shape[-1]).astype(BF)

        return get, 4

    def keep_strips(l, sums):
        for c in range(4):
            y = silu(sums[c]).reshape(2, STRIP, 256)
            if l == 4:
                for side in range(2):
                    for half in range(2):
                        f4[pl.ds(half * COLS + 124 * side + c, 32, 2 * COLS), :] = (
                            y[side, 0:32, half * 128:half * 128 + 128]
                        )
                continue
            y = jnp.where(inside(l, 0, (1, STRIP, 256), 1), y, 0.0)
            for side in range(2):
                sfs[l][side, 2 * side + c, 0:STRIP, :] = y[side]

    for l in range(1, 5):
        top, bottom, sides = product(l, [of_main(l, 0, 2), of_main(l, 34 - l, 2), of_strips(l)])
        keep(l, 0, 2, top, True)
        keep(l, 34 - l, 2, bottom, True)
        keep_strips(l, sides)

    @pl.loop(0, 16, unroll=2)
    def _(tr):
        for u in range(4):
            row = pl.multiple_of((tr * 4 + u) * COLS, COLS)
            fo[tr * 4 + u] = f4[pl.ds(row, COLS), :].astype(BF)
            for b2 in range(2):
                at = pl.multiple_of(tr * 32 + b2 * 16, 16)
                for v in range(4):
                    two = [f4[pl.ds(row + 4 * (2 * b2 + b) + v, 8, 16), :] for b in range(2)]
                    lane = (u * 4 + v) * 128
                    tok[pl.ds(at, 16), lane:lane + 128] = jnp.concatenate(two, axis=0).astype(BF)


def convolve(x, first, rest, embed):
    vm = pl.BlockSpec(memory_space=pltpu.VMEM)
    hb = pl.BlockSpec(memory_space=pltpu.HBM)
    side = pltpu.VMEM((4, 32, 128), BF)
    corner = pltpu.VMEM((16, 128), BF)
    return pl.pallas_call(
        conv_kernel,
        out_shape=(
            jax.ShapeDtypeStruct((64, 128, 128), BF),
            jax.ShapeDtypeStruct((512, 2048), BF),
            jax.ShapeDtypeStruct((2048, 1024), BF),
        ),
        in_specs=[hb, hb, hb, hb],
        out_specs=(vm, vm, vm),
        scratch_shapes=[
            pltpu.VMEM((64, 64, 128), BF),
            pltpu.VMEM((9, 64, 128), BF),
            pltpu.VMEM((27, 128, 128), BF),
            pltpu.VMEM((64 * 64, 128), F32),
            pltpu.VMEM((36, Q, S, 128), BF),
            pltpu.VMEM((35, Q, S, 256), BF),
            pltpu.VMEM((34, Q, S, 256), BF),
            pltpu.VMEM((33, Q, S, 256), BF),
            pltpu.VMEM((64 * 128, 128), F32),
            pltpu.VMEM((768, 256), BF),
            pltpu.VMEM((3, 256, 768), BF),
            pltpu.VMEM((3, 2, 256, 512), BF),
            pltpu.VMEM((2, 4, 32, 128), F32),
            pltpu.VMEM((2, 2, 16, 128), F32),
            pltpu.VMEM((2, 2, 16, 128), BF),
            side, side,
            pltpu.VMEM((2, 6, HELD, 128), F32),
            pltpu.VMEM((2, 6, HELD, 256), F32),
            pltpu.VMEM((2, 6, HELD, 256), F32),
            pltpu.VMEM((2, 6, HELD, 256), F32),
            side, side, corner, corner, corner, corner,
            pltpu.SemaphoreType.DMA((8,)),
            pltpu.SemaphoreType.DMA((8,)),
            pltpu.SemaphoreType.DMA((4,)),
        ],
        compiler_params=pltpu.CompilerParams(
            collective_id=0, has_side_effects=True, vmem_limit_bytes=40 * 2**20
        ),
        name="convolve",
    )(*in_hbm(x, first, rest, embed))


def token_kernel(tok, fo, embed_v, count_ref, patch_hbm, pos_hbm, mix_hbm, head_hbm, up_hbm, down_hbm,
                 feat_hbm, score_ref, patch_ref, pos_ref, mix_ref, head_ref,
                 up_v, down_v, tokens_v, normed_v, hidden_v, pooled_v, sc_v, wsem, fsem):
    pairs = (
        (pos_hbm, pos_ref), (up_hbm, up_v), (down_hbm, down_v), (mix_hbm, mix_ref),
        (head_hbm, head_ref), (patch_hbm, patch_ref),
    )
    loads = [pltpu.make_async_copy(src, dst, wsem.at[i]) for i, (src, dst) in enumerate(pairs)]
    for i in (0, 3, 4, 5, 1, 2):
        loads[i].start()
    feat_copy = pltpu.make_async_copy(fo, feat_hbm, fsem)
    feat_copy.start()

    loads[0].wait()
    loads[3].wait()
    ti = lax.broadcasted_iota(jnp.int32, (128, 16), 0) // 8
    tj = lax.broadcasted_iota(jnp.int32, (128, 16), 1)
    pick = (ti == tj).astype(BF)
    spread = jnp.dot(pick, mix_ref[...], preferred_element_type=F32).astype(BF)
    spread = lax.dot_general(spread, pick, NEG, preferred_element_type=F32)
    ri = lax.broadcasted_iota(jnp.int32, (128, 128), 0) % 8
    rj = lax.broadcasted_iota(jnp.int32, (128, 128), 1) % 8
    mix = jnp.where(ri == rj, spread, 0.0).astype(BF)

    def embed(h):
        rows = slice(h * 256, h * 256 + 256)
        summed = jnp.dot(tok[rows, :], embed_v[...], preferred_element_type=F32)
        wide = summed.reshape(2, 16, 8, 1024) + pos_ref[...].astype(F32)[None, :, None, :]
        tokens_v[rows, :] = wide.reshape(256, 1024).astype(BF)

    def mixes(h):
        for pi in (2 * h, 2 * h + 1):
            rows = slice(pi * 128, pi * 128 + 128)
            wide = tokens_v[rows, :].astype(F32)
            mixing = jnp.dot(mix, norm(wide).astype(BF), preferred_element_type=F32)
            mixed = (wide + mixing).astype(BF)
            tokens_v[rows, :] = mixed
            normed_v[rows, :] = norm(mixed.astype(F32)).astype(BF)

    def widen(h, n):
        rows = slice(h * 256, h * 256 + 256)
        lanes = pl.ds(pl.multiple_of(n * 1024, 1024), 1024)
        hidden = jnp.dot(normed_v[rows, :], up_v[:, lanes], preferred_element_type=F32)
        hidden_v[rows, lanes] = gelu(hidden)

    def narrow(h):
        rows = slice(h * 256, h * 256 + 256)
        summed = jnp.dot(hidden_v[rows, :], down_v[...], preferred_element_type=F32)
        encoded = norm(tokens_v[rows, :].astype(F32) + summed)
        total = jnp.sum(encoded.reshape(2, 16, 8, 1024), axis=1)
        pooled_v[h * 16:h * 16 + 16, :] = total.reshape(16, 1024) * 0.0625

    embed(0)
    embed(1)
    mixes(0)
    loads[1].wait()
    widen(0, 0)
    mixes(1)

    @pl.loop(1, 4, unroll=3)
    def _(n):
        widen(0, n)

    @pl.loop(0, 4, unroll=4)
    def _(n):
        widen(1, n)

    loads[2].wait()
    narrow(0)
    narrow(1)

    for load in loads[4:]:
        load.wait()
    sc_v[0, :, 0:8] = lax.dot_general(
        pooled_v[...].astype(BF), head_ref[...], NEG, preferred_element_type=F32
    )
    for s in range(32):
        line = sc_v[0, pl.ds(patch_ref[0, 0, s], 1), :]
        sc_v[1, pl.ds(s, 1), :] = jnp.where(s < count_ref[0, 0], line, 0.0)
    score_ref[...] = jnp.transpose(sc_v[1], (1, 0))[0:8]
    feat_copy.wait()


def classify(tok, fo, embed, patch, count, pos, mix, head, up, down):
    vm = pl.BlockSpec(memory_space=pltpu.VMEM)
    hb = pl.BlockSpec(memory_space=pltpu.HBM)
    return pl.pallas_call(
        token_kernel,
        out_shape=(
            jax.ShapeDtypeStruct((64, 128, 128), BF),
            jax.ShapeDtypeStruct((8, 32), F32),
        ),
        in_specs=[vm, vm, vm, pl.BlockSpec(memory_space=pltpu.SMEM)] + [hb] * 6,
        out_specs=(hb, vm),
        scratch_shapes=[
            pltpu.SMEM((1, 1, 32), jnp.int32),
            pltpu.VMEM((16, 1024), BF),
            pltpu.VMEM((16, 16), BF),
            pltpu.VMEM((8, 1024), BF),
            pltpu.VMEM((1024, 4096), BF),
            pltpu.VMEM((4096, 1024), BF),
            pltpu.VMEM((512, 1024), BF),
            pltpu.VMEM((512, 1024), BF),
            pltpu.VMEM((512, 4096), BF),
            pltpu.VMEM((32, 1024), F32),
            pltpu.VMEM((2, 32, 128), F32),
            pltpu.SemaphoreType.DMA((6,)),
            pltpu.SemaphoreType.DMA,
        ],
        compiler_params=pltpu.CompilerParams(vmem_limit_bytes=40 * 2**20),
        name="classify",
    )(tok, fo, embed, count, *in_hbm(patch, pos, mix, head, up, down))


def in_hbm(*arrays):
    return tuple(pltpu.with_memory_space_constraint(a, pltpu.HBM) for a in arrays)


def on_device(input_field, conv_first, conv_rest, flag_patch, flag_count, w_embed, pos_embed,
              token_mix, w_up, w_down, w_head):
    fo, tok, embed = convolve(
        input_field, jnp.transpose(conv_first, (0, 1, 3, 2)).reshape(9, 64, 128),
        conv_rest.reshape(27, 128, 128), w_embed,
    )
    features, scores = classify(
        tok, fo, embed, flag_patch, flag_count, pos_embed, token_mix, w_head.T, w_up, w_down,
    )
    return (features, scores.T[None, None])


def solution(mesh):
    placed = (
        P(None, "lat", "lon"), P(), P(), P("lat", "lon", None), P("lat", "lon"),
        P(), P(), P(), P(), P(), P(),
    )
    return jax.shard_map(
        on_device,
        mesh=mesh,
        in_specs=placed,
        out_specs=(P("lat", "lon", None), P("lat", "lon", None, None)),
        check_vma=False,
    )
```

```python
import functools

import jax
import jax.numpy as jnp
from jax import lax
from jax.experimental import pallas as pl
from jax.experimental.pallas import tpu as pltpu
from jax.sharding import PartitionSpec as P

BF = jnp.bfloat16
F32 = jnp.float32
MESH = pl.DeviceIdType.MESH

W = 8
Q = W + 2
S = 16
COLS = W * S
STRIP = 40
HELD = 48
NEG = (((1,), (1,)), ((), ()))
POS = (((1,), (0,)), ((), ()))


def silu(v):
    half = 0.5 * v
    return half + half * jnp.tanh(half)


def gelu(v):
    v = v.astype(BF)
    half = BF(0.5) * v
    return half + half * jnp.tanh(v * (BF(0.7978845608028654) + BF(0.035677408136300125) * (v * v)))


def norm(v):
    centred = v - jnp.mean(v, axis=-1, keepdims=True)
    return centred * lax.rsqrt(jnp.mean(centred * centred, axis=-1, keepdims=True) + 1e-05)


def conv_kernel(x_hbm, first_hbm, rest_hbm, embed_hbm, f4, embed_v, x_ref, first_ref, rest_ref, xf, x0, x1, x2, x3, wt1, wm, we,
                colf, cornf, corner, col_l, col_r, sf0, sf1, sf2, sf3, r_right, r_left, r_br, r_bl, r_tr, r_tl,
                send_sem, recv_sem, load_sem):
    loads = [
        pltpu.make_async_copy(x_hbm, x_ref, load_sem.at[0]),
        pltpu.make_async_copy(first_hbm, first_ref, load_sem.at[1]),
        pltpu.make_async_copy(rest_hbm, rest_ref, load_sem.at[2]),
        pltpu.make_async_copy(embed_hbm, embed_v, load_sem.at[3]),
    ]
    for load in loads[:3]:
        load.start()
    lon = lax.axis_index("lon")
    lat = lax.axis_index("lat")
    n_lon = lax.axis_size("lon")
    n_lat = lax.axis_size("lat")
    west = lax.rem(lon + n_lon - 1, n_lon)
    east = lax.rem(lon + 1, n_lon)
    north = lax.rem(lat + n_lat - 1, n_lat)
    south = lax.rem(lat + 1, n_lat)
    barrier = pltpu.get_barrier_semaphore()
    places = ((lon, north), (lon, south), (west, lat), (east, lat),
              (west, north), (east, north), (west, south), (east, south))
    for place in places:
        pl.semaphore_signal(barrier, inc=1, device_id=place, device_id_type=MESH)
    low = jnp.where(lat == 0, 0, -64)
    high = jnp.where(lat == n_lat - 1, 64, 128)

    loads[0].wait()
    xf[...] = x_ref[...].astype(F32).reshape(64 * 64, 128)
    mm = lax.broadcasted_iota(jnp.int32, (Q * S, 128), 0)
    jj = lax.broadcasted_iota(jnp.int32, (Q * S, 128), 1)
    order = (jj == mm % S * W + mm // S - 1).astype(BF)

    def turn(k):
        rows = jnp.concatenate(
            [xf[pl.ds(2 * k + i, 64, 64), :] for i in range(4)], axis=0
        ).astype(BF)
        cells = lax.dot_general(order, rows, NEG, preferred_element_type=F32)
        for h in range(2):
            own = cells[:, h * 128:h * 128 + 128].reshape(Q, S, 128)
            x0[k + 2 + h] = own.astype(BF)
            for c in range(4):
                colf[0, c, pl.ds(k + h, 1), :] = own[c + 1, 0:1]
                colf[1, c, pl.ds(k + h, 1), :] = own[c + 5, 15:16]
            for c in range(2):
                sf0[0, 4 + c, pl.ds(k + 2 + h, 1), :] = own[c + 1, 0:1]
                sf0[1, c, pl.ds(k + 2 + h, 1), :] = own[c + 7, 15:16]

    @pl.loop(0, 16, unroll=4)
    def _(k):
        turn(2 * k)

    cornf[...] = jnp.zeros((2, 2, 16, 128), F32)
    for e in range(2):
        for end in range(2):
            for c in range(4):
                cornf[e, end, 2 * c:2 * c + 2, :] = colf[e, c, 30 * end:30 * end + 2, :]
    corner[...] = cornf[...].astype(BF)
    col_l[...] = colf[0].astype(BF)
    col_r[...] = colf[1].astype(BF)

    loads[1].wait()
    loads[2].wait()
    loads[3].start()
    for ro in range(2):
        out = slice(ro * 128, ro * 128 + 128)
        for p in range(2):
            for dq in range(3):
                for half in range(2):
                    a = 2 * p + half - ro
                    at = (p * 3 + dq) * 2 + half
                    wt1[at * 64:at * 64 + 64, out] = (
                        first_ref[a * 3 + dq] if 0 <= a < 3 else jnp.zeros((64, 128), BF)
                    )
    for l in range(3):
        for o in range(2):
            out = slice(o * 128, o * 128 + 128)
            for dq in range(3):
                for i in range(2):
                    at = (dq * 2 + i) * 128
                    wm[l, out, at:at + 128] = rest_ref[l * 9 + (i + 1 - o) * 3 + dq]
            for e in range(2):
                for t in range(4):
                    b = t - o
                    we[l, e, out, t * 128:t * 128 + 128] = (
                        rest_ref[l * 9 + 6 * e + b] if 0 <= b < 3 else jnp.zeros((128, 128), BF)
                    )

    xs = (x0, x1, x2, x3)
    sfs = (sf0, sf1, sf2, sf3)

    def product(l, groups):
        def stack(p, first, step, *half):
            return jnp.concatenate(
                [get(p, c, *half) for get, n in groups for c in range(first, first + n, step)], axis=0
            )

        def split(whole, parts):
            at = 0
            for size, n in parts:
                yield [whole[at + c * size:at + c * size + size] for c in range(n)]
                at += size * n

        sizes = [(get(0, 0).shape[0], n) for get, n in groups]
        if l == 1:
            slabs = [stack(p, dq, 1) for p in range(2) for dq in range(3)]
            full = jnp.dot(jnp.concatenate(slabs, axis=1), wt1[...], preferred_element_type=F32)
            return list(split(full, sizes))
        slabs = []
        for dq in range(3):
            slabs += [stack(0, dq, 1, 1), stack(1, dq, 1, 0)]
        full = lax.dot_general(jnp.concatenate(slabs, axis=1), wm[l - 2], NEG, preferred_element_type=F32)
        outer = []
        for e in range(2):
            slabs = [stack(e, t, 2, e) for t in range(4)]
            part = lax.dot_general(
                jnp.concatenate(slabs, axis=1), we[l - 2, e], NEG, preferred_element_type=F32
            )
            outer.append(list(split(part, [(size, n // 2) for size, n in sizes])))
        sums = []
        for g, columns in enumerate(split(full, sizes)):
            for c in range(len(columns)):
                lanes = slice(c % 2 * 128, c % 2 * 128 + 128)
                columns[c] = columns[c] + jnp.concatenate(
                    [part[g][c // 2][:, lanes] for part in outer], axis=1
                )
            sums.append(columns)
        return sums

    def inside(l, first, shape, dim):
        pair = lax.broadcasted_iota(jnp.int32, shape, dim)
        lane = lax.broadcasted_iota(jnp.int32, shape, len(shape) - 1)
        row = l - 4 + 2 * (first + pair) + lane // 128
        return (row >= low) & (row < high)

    def of_main(l, k, r):
        src = xs[l - 1]

        def get(p, c, half=None):
            lanes = slice(None) if half is None else slice(half * 128, half * 128 + 128)
            part = src[pl.ds(k + p, r), c, :, lanes]
            return part.reshape(r * S, part.shape[-1])

        return get, W

    def keep(l, k, r, sums, border=False):
        for q in range(W):
            y = silu(sums[q]).reshape(r, S, 256)
            if border and l < 4:
                y = jnp.where(inside(l, k, (r, S, 256), 0), y, 0.0)
            if l == 4:
                for i in range(r):
                    for half in range(2):
                        f4[pl.ds((2 * (k + i) + half) * COLS + q, S, W), :] = (
                            y[i, :, half * 128:half * 128 + 128]
                        )
                continue
            dst = xs[l]
            dst[pl.ds(k, r), q + 1] = y.astype(BF)
            for i in range(r):
                if q == W - 1:
                    dst[k + i, 0] = pltpu.roll(y[i], 1, 0).astype(BF)
                if q == 0:
                    dst[k + i, W + 1] = pltpu.roll(y[i], S - 1, 0).astype(BF)
                for c in range(2):
                    if q == l + c:
                        sfs[l][0, 4 + c, pl.ds(k + i, 1), :] = y[i, 0:1]
                    if q == W - 2 - l + c:
                        sfs[l][1, c, pl.ds(k + i, 1), :] = y[i, S - 1:S]

    def inner(l, r, first=0, last=None):
        pairs = 32 - l
        steps = (pairs + r - 1) // r

        @pl.loop(first, steps if last is None else last)
        def _(step):
            k = jnp.minimum(2 + step * r, 2 + pairs - r)
            keep(l, k, r, product(l, [of_main(l, k, r)])[0])

    inner(1, 16, 0, 1)

    pl.semaphore_wait(barrier, 8)
    sends = (
        (x0.at[2:4, 1:W + 1], x0.at[34:36, 1:W + 1]), (x0.at[32:34, 1:W + 1], x0.at[0:2, 1:W + 1]),
        (col_l, r_right), (col_r, r_left), (corner.at[0, 0], r_br), (corner.at[1, 0], r_bl),
        (corner.at[0, 1], r_tr), (corner.at[1, 1], r_tl),
    )
    copies = []
    for i, ((src, dst), place) in enumerate(zip(sends, places)):
        copies.append(pltpu.make_async_remote_copy(
            src_ref=src, dst_ref=dst, send_sem=send_sem.at[i], recv_sem=recv_sem.at[i],
            device_id=place, device_id_type=MESH,
        ))
        copies[-1].start()

    inner(1, 16, 1)
    inner(2, 15)
    inner(3, 15)
    inner(4, 14)

    loads[3].wait()
    for copy in copies:
        copy.wait()

    @pl.when(lat == 0)
    def _():
        x0[0:2] = jnp.zeros((2, Q, S, 128), BF)

    @pl.when(lat == n_lat - 1)
    def _():
        x0[34:36] = jnp.zeros((2, Q, S, 128), BF)

    sf0[0, 0:4, 2:34, :] = r_left[...].astype(F32)
    sf0[1, 2:6, 2:34, :] = r_right[...].astype(F32)
    for at, west_end, east_end in ((0, r_tl, r_tr), (34, r_bl, r_br)):
        for e, end in enumerate((west_end, east_end)):
            rows = end[...].astype(F32)
            for c in range(4):
                sf0[e, 2 * e + c, at:at + 2, :] = rows[2 * c:2 * c + 2]
        for k in (at, at + 1):
            first = x0[k, 1].astype(F32)
            last = x0[k, W].astype(F32)
            x0[k, 0] = pltpu.roll(last, 1, 0).astype(BF)
            x0[k, W + 1] = pltpu.roll(first, S - 1, 0).astype(BF)
            sf0[0, 4, k:k + 1, :] = first[0:1]
            sf0[0, 5, k:k + 1, :] = x0[k, 2].astype(F32)[0:1]
            sf0[1, 0, k:k + 1, :] = x0[k, W - 1].astype(F32)[S - 1:S]
            sf0[1, 1, k:k + 1, :] = last[S - 1:S]

    @pl.when(lat == 0)
    def _():
        sf0[:, :, 0:2, :] = jnp.zeros((2, 6, 2, 128), F32)

    @pl.when(lat == n_lat - 1)
    def _():
        sf0[:, :, 34:36, :] = jnp.zeros((2, 6, 2, 128), F32)

    def of_strips(l):
        src = sfs[l - 1]

        def get(p, c, half=None):
            lanes = slice(None) if half is None else slice(half * 128, half * 128 + 128)
            part = src[:, c, p:p + STRIP, lanes]
            return part.reshape(2 * STRIP, part.shape[-1]).astype(BF)

        return get, 4

    def keep_strips(l, sums):
        for c in range(4):
            y = silu(sums[c]).reshape(2, STRIP, 256)
            if l == 4:
                for side in range(2):
                    for half in range(2):
                        f4[pl.ds(half * COLS + 124 * side + c, 32, 2 * COLS), :] = (
                            y[side, 0:32, half * 128:half * 128 + 128]
                        )
                continue
            y = jnp.where(inside(l, 0, (1, STRIP, 256), 1), y, 0.0)
            for side in range(2):
                sfs[l][side, 2 * side + c, 0:STRIP, :] = y[side]

    for l in range(1, 5):
        top, bottom, sides = product(l, [of_main(l, 0, 2), of_main(l, 34 - l, 2), of_strips(l)])
        keep(l, 0, 2, top, True)
        keep(l, 34 - l, 2, bottom, True)
        keep_strips(l, sides)


def convolve(x, first, rest, embed):
    vm = pl.BlockSpec(memory_space=pltpu.VMEM)
    hb = pl.BlockSpec(memory_space=pltpu.HBM)
    side = pltpu.VMEM((4, 32, 128), BF)
    corner = pltpu.VMEM((16, 128), BF)
    return pl.pallas_call(
        conv_kernel,
        out_shape=(
            jax.ShapeDtypeStruct((64 * 128, 128), F32),
            jax.ShapeDtypeStruct((2048, 1024), BF),
        ),
        in_specs=[hb, hb, hb, hb],
        out_specs=(vm, vm),
        scratch_shapes=[
            pltpu.VMEM((64, 64, 128), BF),
            pltpu.VMEM((9, 64, 128), BF),
            pltpu.VMEM((27, 128, 128), BF),
            pltpu.VMEM((64 * 64, 128), F32),
            pltpu.VMEM((36, Q, S, 128), BF),
            pltpu.VMEM((35, Q, S, 256), BF),
            pltpu.VMEM((34, Q, S, 256), BF),
            pltpu.VMEM((33, Q, S, 256), BF),
            pltpu.VMEM((768, 256), BF),
            pltpu.VMEM((3, 256, 768), BF),
            pltpu.VMEM((3, 2, 256, 512), BF),
            pltpu.VMEM((2, 4, 32, 128), F32),
            pltpu.VMEM((2, 2, 16, 128), F32),
            pltpu.VMEM((2, 2, 16, 128), BF),
            side, side,
            pltpu.VMEM((2, 6, HELD, 128), F32),
            pltpu.VMEM((2, 6, HELD, 256), F32),
            pltpu.VMEM((2, 6, HELD, 256), F32),
            pltpu.VMEM((2, 6, HELD, 256), F32),
            side, side, corner, corner, corner, corner,
            pltpu.SemaphoreType.DMA((8,)),
            pltpu.SemaphoreType.DMA((8,)),
            pltpu.SemaphoreType.DMA((4,)),
        ],
        compiler_params=pltpu.CompilerParams(
            collective_id=0, has_side_effects=True, vmem_limit_bytes=40 * 2**20
        ),
        name="convolve",
    )(*in_hbm(x, first, rest, embed))


def token_kernel(f4, embed_v, count_ref, patch_hbm, pos_hbm, mix_hbm, head_hbm, up_hbm, down_hbm,
                 feat_hbm, score_ref, patch_ref, pos_ref, mix_ref, head_ref,
                 fo, tok, up_v, down_v, tokens_v, normed_v, hidden_v, pooled_v, sc_v, wsem, fsem):
    pairs = (
        (pos_hbm, pos_ref), (up_hbm, up_v), (down_hbm, down_v), (mix_hbm, mix_ref),
        (head_hbm, head_ref), (patch_hbm, patch_ref),
    )
    loads = [pltpu.make_async_copy(src, dst, wsem.at[i]) for i, (src, dst) in enumerate(pairs)]
    for i in (0, 3, 4, 5, 1):
        loads[i].start()
    feat_copy = pltpu.make_async_copy(fo, feat_hbm, fsem)

    def gather(h):
        for tr in range(8 * h, 8 * h + 8):
            for u in range(4):
                row = (tr * 4 + u) * COLS
                fo[tr * 4 + u] = f4[row:row + COLS, :].astype(BF)
                for b2 in range(2):
                    at = tr * 32 + b2 * 16
                    for v in range(4):
                        two = [f4[pl.ds(row + 4 * (2 * b2 + b) + v, 8, 16), :] for b in range(2)]
                        lane = (u * 4 + v) * 128
                        tok[at:at + 16, lane:lane + 128] = jnp.concatenate(two, axis=0).astype(BF)

    loads[0].wait()
    loads[3].wait()
    ti = lax.broadcasted_iota(jnp.int32, (128, 16), 0) // 8
    tj = lax.broadcasted_iota(jnp.int32, (128, 16), 1)
    pick = (ti == tj).astype(BF)
    spread = jnp.dot(pick, mix_ref[...], preferred_element_type=F32).astype(BF)
    spread = lax.dot_general(spread, pick, NEG, preferred_element_type=F32)
    ri = lax.broadcasted_iota(jnp.int32, (128, 128), 0) % 8
    rj = lax.broadcasted_iota(jnp.int32, (128, 128), 1) % 8
    mix = jnp.where(ri == rj, spread, 0.0).astype(BF)

    def embed(h):
        rows = slice(h * 256, h * 256 + 256)
        summed = jnp.dot(tok[rows, :], embed_v[...], preferred_element_type=F32)
        wide = summed.reshape(2, 16, 8, 1024) + pos_ref[...].astype(F32)[None, :, None, :]
        tokens_v[rows, :] = wide.reshape(256, 1024).astype(BF)

    def mixes(h):
        for pi in (2 * h, 2 * h + 1):
            rows = slice(pi * 128, pi * 128 + 128)
            wide = tokens_v[rows, :].astype(F32)
            mixing = jnp.dot(mix, norm(wide).astype(BF), preferred_element_type=F32)
            mixed = (wide + mixing).astype(BF)
            tokens_v[rows, :] = mixed
            normed_v[rows, :] = norm(mixed.astype(F32)).astype(BF)

    def widen(h, n):
        rows = slice(h * 256, h * 256 + 256)
        lanes = pl.ds(pl.multiple_of(n * 1024, 1024), 1024)
        hidden = jnp.dot(normed_v[rows, :], up_v[:, lanes], preferred_element_type=F32)
        hidden_v[rows, lanes] = gelu(hidden)

    def narrow(h):
        rows = slice(h * 256, h * 256 + 256)
        summed = jnp.dot(hidden_v[rows, :], down_v[...], preferred_element_type=F32)
        encoded = norm(tokens_v[rows, :].astype(F32) + summed)
        total = jnp.sum(encoded.reshape(2, 16, 8, 1024), axis=1)
        pooled_v[h * 16:h * 16 + 16, :] = total.reshape(16, 1024) * 0.0625

    gather(0)
    embed(0)
    gather(1)
    embed(1)
    mixes(0)
    loads[1].wait()
    loads[2].start()
    feat_copy.start()
    widen(0, 0)
    mixes(1)

    @pl.loop(1, 4, unroll=3)
    def _(n):
        widen(0, n)

    @pl.loop(0, 4, unroll=4)
    def _(n):
        widen(1, n)

    loads[2].wait()
    narrow(0)
    narrow(1)

    for load in loads[4:]:
        load.wait()
    sc_v[0, :, 0:8] = lax.dot_general(
        pooled_v[...].astype(BF), head_ref[...], NEG, preferred_element_type=F32
    )
    for s in range(32):
        line = sc_v[0, pl.ds(patch_ref[0, 0, s], 1), :]
        sc_v[1, pl.ds(s, 1), :] = jnp.where(s < count_ref[0, 0], line, 0.0)
    score_ref[...] = jnp.transpose(sc_v[1], (1, 0))[0:8]
    feat_copy.wait()


def classify(f4, embed, patch, count, pos, mix, head, up, down):
    vm = pl.BlockSpec(memory_space=pltpu.VMEM)
    hb = pl.BlockSpec(memory_space=pltpu.HBM)
    return pl.pallas_call(
        token_kernel,
        out_shape=(
            jax.ShapeDtypeStruct((64, 128, 128), BF),
            jax.ShapeDtypeStruct((8, 32), F32),
        ),
        in_specs=[vm, vm, pl.BlockSpec(memory_space=pltpu.SMEM)] + [hb] * 6,
        out_specs=(hb, vm),
        scratch_shapes=[
            pltpu.SMEM((1, 1, 32), jnp.int32),
            pltpu.VMEM((16, 1024), BF),
            pltpu.VMEM((16, 16), BF),
            pltpu.VMEM((8, 1024), BF),
            pltpu.VMEM((64, 128, 128), BF),
            pltpu.VMEM((512, 2048), BF),
            pltpu.VMEM((1024, 4096), BF),
            pltpu.VMEM((4096, 1024), BF),
            pltpu.VMEM((512, 1024), BF),
            pltpu.VMEM((512, 1024), BF),
            pltpu.VMEM((512, 4096), BF),
            pltpu.VMEM((32, 1024), F32),
            pltpu.VMEM((2, 32, 128), F32),
            pltpu.SemaphoreType.DMA((6,)),
            pltpu.SemaphoreType.DMA,
        ],
        compiler_params=pltpu.CompilerParams(vmem_limit_bytes=40 * 2**20),
        name="classify",
    )(f4, embed, count, *in_hbm(patch, pos, mix, head, up, down))


def in_hbm(*arrays):
    return tuple(pltpu.with_memory_space_constraint(a, pltpu.HBM) for a in arrays)


def on_device(input_field, conv_first, conv_rest, flag_patch, flag_count, w_embed, pos_embed,
              token_mix, w_up, w_down, w_head):
    f4, embed = convolve(
        input_field, jnp.transpose(conv_first, (0, 1, 3, 2)).reshape(9, 64, 128),
        conv_rest.reshape(27, 128, 128), w_embed,
    )
    features, scores = classify(
        f4, embed, flag_patch, flag_count, pos_embed, token_mix, w_head.T, w_up, w_down,
    )
    return (features, scores.T[None, None])


def solution(mesh):
    placed = (
        P(None, "lat", "lon"), P(), P(), P("lat", "lon", None), P("lat", "lon"),
        P(), P(), P(), P(), P(), P(),
    )
    return jax.shard_map(
        on_device,
        mesh=mesh,
        in_specs=placed,
        out_specs=(P("lat", "lon", None), P("lat", "lon", None, None)),
        check_vma=False,
    )
```

```python
import functools

import jax
import jax.numpy as jnp
from jax import lax
from jax.experimental import pallas as pl
from jax.experimental.pallas import tpu as pltpu
from jax.sharding import PartitionSpec as P

BF = jnp.bfloat16
F32 = jnp.float32
MESH = pl.DeviceIdType.MESH

W = 8
Q = W + 2
S = 16
COLS = W * S
STRIP = 40
HELD = 48
NEG = (((1,), (1,)), ((), ()))
POS = (((1,), (0,)), ((), ()))


def silu(v):
    half = 0.5 * v
    return half + half * jnp.tanh(half)


def gelu(v):
    v = v.astype(BF)
    half = BF(0.5) * v
    return half + half * jnp.tanh(v * (BF(0.7978845608028654) + BF(0.035677408136300125) * (v * v)))


def norm(v):
    centred = v - jnp.mean(v, axis=-1, keepdims=True)
    return centred * lax.rsqrt(jnp.mean(centred * centred, axis=-1, keepdims=True) + 1e-05)


def conv_kernel(x_hbm, first_hbm, rest_hbm, embed_hbm, f4, embed_v, x_ref, first_ref, rest_ref, xf, x0, x1, x2, x3, wt1, wm, we,
                colf, cornf, corner, col_l, col_r, sf0, sf1, sf2, sf3, r_right, r_left, r_br, r_bl, r_tr, r_tl,
                send_sem, recv_sem, load_sem):
    loads = [
        pltpu.make_async_copy(x_hbm, x_ref, load_sem.at[0]),
        pltpu.make_async_copy(first_hbm, first_ref, load_sem.at[1]),
        pltpu.make_async_copy(rest_hbm, rest_ref, load_sem.at[2]),
        pltpu.make_async_copy(embed_hbm, embed_v, load_sem.at[3]),
    ]
    for load in loads[:3]:
        load.start()
    lon = lax.axis_index("lon")
    lat = lax.axis_index("lat")
    n_lon = lax.axis_size("lon")
    n_lat = lax.axis_size("lat")
    west = lax.rem(lon + n_lon - 1, n_lon)
    east = lax.rem(lon + 1, n_lon)
    north = lax.rem(lat + n_lat - 1, n_lat)
    south = lax.rem(lat + 1, n_lat)
    barrier = pltpu.get_barrier_semaphore()
    places = ((lon, north), (lon, south), (west, lat), (east, lat),
              (west, north), (east, north), (west, south), (east, south))
    to_north, to_south, level = (0, 4, 5), (1, 6, 7), (2, 3)
    has_north, has_south = lat > 0, lat < n_lat - 1

    def greet(those):
        for i in those:
            pl.semaphore_signal(barrier, inc=1, device_id=places[i], device_id_type=MESH)

    greet(level)
    pl.when(has_north)(lambda: greet(to_north))
    pl.when(has_south)(lambda: greet(to_south))
    low = jnp.where(lat == 0, 0, -64)
    high = jnp.where(lat == n_lat - 1, 64, 128)

    loads[0].wait()
    xf[...] = x_ref[...].astype(F32).reshape(64 * 64, 128)
    mm = lax.broadcasted_iota(jnp.int32, (Q * S, 128), 0)
    jj = lax.broadcasted_iota(jnp.int32, (Q * S, 128), 1)
    order = (jj == mm % S * W + mm // S - 1).astype(BF)

    def turn(k):
        rows = jnp.concatenate(
            [xf[pl.ds(2 * k + i, 64, 64), :] for i in range(4)], axis=0
        ).astype(BF)
        cells = lax.dot_general(order, rows, NEG, preferred_element_type=F32)
        for h in range(2):
            own = cells[:, h * 128:h * 128 + 128].reshape(Q, S, 128)
            x0[k + 2 + h] = own.astype(BF)
            for c in range(4):
                colf[0, c, pl.ds(k + h, 1), :] = own[c + 1, 0:1]
                colf[1, c, pl.ds(k + h, 1), :] = own[c + 5, 15:16]
            for c in range(2):
                sf0[0, 4 + c, pl.ds(k + 2 + h, 1), :] = own[c + 1, 0:1]
                sf0[1, c, pl.ds(k + 2 + h, 1), :] = own[c + 7, 15:16]

    @pl.loop(0, 16, unroll=4)
    def _(k):
        turn(2 * k)

    cornf[...] = jnp.zeros((2, 2, 16, 128), F32)
    for e in range(2):
        for end in range(2):
            for c in range(4):
                cornf[e, end, 2 * c:2 * c + 2, :] = colf[e, c, 30 * end:30 * end + 2, :]
    corner[...] = cornf[...].astype(BF)
    col_l[...] = colf[0].astype(BF)
    col_r[...] = colf[1].astype(BF)

    loads[1].wait()
    loads[2].wait()
    loads[3].start()
    for ro in range(2):
        out = slice(ro * 128, ro * 128 + 128)
        for p in range(2):
            for dq in range(3):
                for half in range(2):
                    a = 2 * p + half - ro
                    at = (p * 3 + dq) * 2 + half
                    wt1[at * 64:at * 64 + 64, out] = (
                        first_ref[a * 3 + dq] if 0 <= a < 3 else jnp.zeros((64, 128), BF)
                    )
    for l in range(3):
        for o in range(2):
            out = slice(o * 128, o * 128 + 128)
            for dq in range(3):
                for i in range(2):
                    at = (dq * 2 + i) * 128
                    wm[l, out, at:at + 128] = rest_ref[l * 9 + (i + 1 - o) * 3 + dq]
            for e in range(2):
                for t in range(4):
                    b = t - o
                    we[l, e, out, t * 128:t * 128 + 128] = (
                        rest_ref[l * 9 + 6 * e + b] if 0 <= b < 3 else jnp.zeros((128, 128), BF)
                    )

    xs = (x0, x1, x2, x3)
    sfs = (sf0, sf1, sf2, sf3)

    def product(l, groups):
        def stack(p, first, step, *half):
            return jnp.concatenate(
                [get(p, c, *half) for get, n in groups for c in range(first, first + n, step)], axis=0
            )

        def split(whole, parts):
            at = 0
            for size, n in parts:
                yield [whole[at + c * size:at + c * size + size] for c in range(n)]
                at += size * n

        sizes = [(get(0, 0).shape[0], n) for get, n in groups]
        if l == 1:
            slabs = [stack(p, dq, 1) for p in range(2) for dq in range(3)]
            full = jnp.dot(jnp.concatenate(slabs, axis=1), wt1[...], preferred_element_type=F32)
            return list(split(full, sizes))
        slabs = []
        for dq in range(3):
            slabs += [stack(0, dq, 1, 1), stack(1, dq, 1, 0)]
        full = lax.dot_general(jnp.concatenate(slabs, axis=1), wm[l - 2], NEG, preferred_element_type=F32)
        outer = []
        for e in range(2):
            slabs = [stack(e, t, 2, e) for t in range(4)]
            part = lax.dot_general(
                jnp.concatenate(slabs, axis=1), we[l - 2, e], NEG, preferred_element_type=F32
            )
            outer.append(list(split(part, [(size, n // 2) for size, n in sizes])))
        sums = []
        for g, columns in enumerate(split(full, sizes)):
            for c in range(len(columns)):
                lanes = slice(c % 2 * 128, c % 2 * 128 + 128)
                columns[c] = columns[c] + jnp.concatenate(
                    [part[g][c // 2][:, lanes] for part in outer], axis=1
                )
            sums.append(columns)
        return sums

    def inside(l, first, shape, dim):
        pair = lax.broadcasted_iota(jnp.int32, shape, dim)
        lane = lax.broadcasted_iota(jnp.int32, shape, len(shape) - 1)
        row = l - 4 + 2 * (first + pair) + lane // 128
        return (row >= low) & (row < high)

    def of_main(l, k, r):
        src = xs[l - 1]

        def get(p, c, half=None):
            lanes = slice(None) if half is None else slice(half * 128, half * 128 + 128)
            part = src[pl.ds(k + p, r), c, :, lanes]
            return part.reshape(r * S, part.shape[-1])

        return get, W

    def keep(l, k, r, sums, border=False):
        for q in range(W):
            y = silu(sums[q]).reshape(r, S, 256)
            if border and l < 4:
                y = jnp.where(inside(l, k, (r, S, 256), 0), y, 0.0)
            if l == 4:
                for i in range(r):
                    for half in range(2):
                        f4[pl.ds((2 * (k + i) + half) * COLS + q, S, W), :] = (
                            y[i, :, half * 128:half * 128 + 128]
                        )
                continue
            dst = xs[l]
            dst[pl.ds(k, r), q + 1] = y.astype(BF)
            for i in range(r):
                if q == W - 1:
                    dst[k + i, 0] = pltpu.roll(y[i], 1, 0).astype(BF)
                if q == 0:
                    dst[k + i, W + 1] = pltpu.roll(y[i], S - 1, 0).astype(BF)
                for c in range(2):
                    if q == l + c:
                        sfs[l][0, 4 + c, pl.ds(k + i, 1), :] = y[i, 0:1]
                    if q == W - 2 - l + c:
                        sfs[l][1, c, pl.ds(k + i, 1), :] = y[i, S - 1:S]

    def inner(l, r, first=0, last=None):
        pairs = 32 - l
        steps = (pairs + r - 1) // r

        @pl.loop(first, steps if last is None else last)
        def _(step):
            k = jnp.minimum(2 + step * r, 2 + pairs - r)
            keep(l, k, r, product(l, [of_main(l, k, r)])[0])

    inner(1, 16, 0, 1)

    surrounded = jnp.logical_and(has_north, has_south)
    pl.when(surrounded)(lambda: pl.semaphore_wait(barrier, 8))
    pl.when(jnp.logical_not(surrounded))(lambda: pl.semaphore_wait(barrier, 5))
    sends = (
        (x0.at[2:4, 1:W + 1], x0.at[34:36, 1:W + 1]), (x0.at[32:34, 1:W + 1], x0.at[0:2, 1:W + 1]),
        (col_l, r_right), (col_r, r_left), (corner.at[0, 0], r_br), (corner.at[1, 0], r_bl),
        (corner.at[0, 1], r_tr), (corner.at[1, 1], r_tl),
    )
    copies = []
    for i, ((src, dst), place) in enumerate(zip(sends, places)):
        copies.append(pltpu.make_async_remote_copy(
            src_ref=src, dst_ref=dst, send_sem=send_sem.at[i], recv_sem=recv_sem.at[i],
            device_id=place, device_id_type=MESH,
        ))

    def send(those):
        for i in those:
            copies[i].start()

    def sent(those):
        for i in those:
            copies[i].wait_send()

    def arrived(those):
        for i in those:
            copies[i].wait_recv()

    pl.when(has_north)(lambda: send(to_north))
    pl.when(has_south)(lambda: send(to_south))
    send(level)

    inner(1, 16, 1)
    inner(2, 15)
    inner(3, 15)
    inner(4, 14)

    loads[3].wait()
    sent(level)
    arrived(level)

    @pl.when(has_north)
    def _():
        sent(to_north)
        arrived(to_south)

    @pl.when(has_south)
    def _():
        sent(to_south)
        arrived(to_north)

    @pl.when(lat == 0)
    def _():
        x0[0:2] = jnp.zeros((2, Q, S, 128), BF)

    @pl.when(lat == n_lat - 1)
    def _():
        x0[34:36] = jnp.zeros((2, Q, S, 128), BF)

    sf0[0, 0:4, 2:34, :] = r_left[...].astype(F32)
    sf0[1, 2:6, 2:34, :] = r_right[...].astype(F32)
    for at, west_end, east_end in ((0, r_tl, r_tr), (34, r_bl, r_br)):
        for e, end in enumerate((west_end, east_end)):
            rows = end[...].astype(F32)
            for c in range(4):
                sf0[e, 2 * e + c, at:at + 2, :] = rows[2 * c:2 * c + 2]
        for k in (at, at + 1):
            first = x0[k, 1].astype(F32)
            last = x0[k, W].astype(F32)
            x0[k, 0] = pltpu.roll(last, 1, 0).astype(BF)
            x0[k, W + 1] = pltpu.roll(first, S - 1, 0).astype(BF)
            sf0[0, 4, k:k + 1, :] = first[0:1]
            sf0[0, 5, k:k + 1, :] = x0[k, 2].astype(F32)[0:1]
            sf0[1, 0, k:k + 1, :] = x0[k, W - 1].astype(F32)[S - 1:S]
            sf0[1, 1, k:k + 1, :] = last[S - 1:S]

    @pl.when(lat == 0)
    def _():
        sf0[:, :, 0:2, :] = jnp.zeros((2, 6, 2, 128), F32)

    @pl.when(lat == n_lat - 1)
    def _():
        sf0[:, :, 34:36, :] = jnp.zeros((2, 6, 2, 128), F32)

    def of_strips(l):
        src = sfs[l - 1]

        def get(p, c, half=None):
            lanes = slice(None) if half is None else slice(half * 128, half * 128 + 128)
            part = src[:, c, p:p + STRIP, lanes]
            return part.reshape(2 * STRIP, part.shape[-1]).astype(BF)

        return get, 4

    def keep_strips(l, sums):
        for c in range(4):
            y = silu(sums[c]).reshape(2, STRIP, 256)
            if l == 4:
                for side in range(2):
                    for half in range(2):
                        f4[pl.ds(half * COLS + 124 * side + c, 32, 2 * COLS), :] = (
                            y[side, 0:32, half * 128:half * 128 + 128]
                        )
                continue
            y = jnp.where(inside(l, 0, (1, STRIP, 256), 1), y, 0.0)
            for side in range(2):
                sfs[l][side, 2 * side + c, 0:STRIP, :] = y[side]

    for l in range(1, 5):
        top, bottom, sides = product(l, [of_main(l, 0, 2), of_main(l, 34 - l, 2), of_strips(l)])
        keep(l, 0, 2, top, True)
        keep(l, 34 - l, 2, bottom, True)
        keep_strips(l, sides)


def convolve(x, first, rest, embed):
    vm = pl.BlockSpec(memory_space=pltpu.VMEM)
    hb = pl.BlockSpec(memory_space=pltpu.HBM)
    side = pltpu.VMEM((4, 32, 128), BF)
    corner = pltpu.VMEM((16, 128), BF)
    return pl.pallas_call(
        conv_kernel,
        out_shape=(
            jax.ShapeDtypeStruct((64 * 128, 128), F32),
            jax.ShapeDtypeStruct((2048, 1024), BF),
        ),
        in_specs=[hb, hb, hb, hb],
        out_specs=(vm, vm),
        scratch_shapes=[
            pltpu.VMEM((64, 64, 128), BF),
            pltpu.VMEM((9, 64, 128), BF),
            pltpu.VMEM((27, 128, 128), BF),
            pltpu.VMEM((64 * 64, 128), F32),
            pltpu.VMEM((36, Q, S, 128), BF),
            pltpu.VMEM((35, Q, S, 256), BF),
            pltpu.VMEM((34, Q, S, 256), BF),
            pltpu.VMEM((33, Q, S, 256), BF),
            pltpu.VMEM((768, 256), BF),
            pltpu.VMEM((3, 256, 768), BF),
            pltpu.VMEM((3, 2, 256, 512), BF),
            pltpu.VMEM((2, 4, 32, 128), F32),
            pltpu.VMEM((2, 2, 16, 128), F32),
            pltpu.VMEM((2, 2, 16, 128), BF),
            side, side,
            pltpu.VMEM((2, 6, HELD, 128), F32),
            pltpu.VMEM((2, 6, HELD, 256), F32),
            pltpu.VMEM((2, 6, HELD, 256), F32),
            pltpu.VMEM((2, 6, HELD, 256), F32),
            side, side, corner, corner, corner, corner,
            pltpu.SemaphoreType.DMA((8,)),
            pltpu.SemaphoreType.DMA((8,)),
            pltpu.SemaphoreType.DMA((4,)),
        ],
        compiler_params=pltpu.CompilerParams(
            collective_id=0, has_side_effects=True, vmem_limit_bytes=40 * 2**20
        ),
        name="convolve",
    )(*in_hbm(x, first, rest, embed))


def token_kernel(f4, embed_v, count_ref, patch_hbm, pos_hbm, mix_hbm, head_hbm, up_hbm, down_hbm,
                 feat_hbm, score_ref, patch_ref, pos_ref, mix_ref, head_ref,
                 fo, tok, up_v, down_v, tokens_v, normed_v, hidden_v, pooled_v, sc_v, wsem, fsem):
    pairs = (
        (pos_hbm, pos_ref), (up_hbm, up_v), (down_hbm, down_v), (mix_hbm, mix_ref),
        (head_hbm, head_ref), (patch_hbm, patch_ref),
    )
    loads = [pltpu.make_async_copy(src, dst, wsem.at[i]) for i, (src, dst) in enumerate(pairs)]
    for i in (0, 3, 4, 5, 1):
        loads[i].start()
    feat_copy = pltpu.make_async_copy(fo, feat_hbm, fsem)

    def gather(h):
        for tr in range(8 * h, 8 * h + 8):
            for u in range(4):
                row = (tr * 4 + u) * COLS
                fo[tr * 4 + u] = f4[row:row + COLS, :].astype(BF)
                for b2 in range(2):
                    at = tr * 32 + b2 * 16
                    for v in range(4):
                        two = [f4[pl.ds(row + 4 * (2 * b2 + b) + v, 8, 16), :] for b in range(2)]
                        lane = (u * 4 + v) * 128
                        tok[at:at + 16, lane:lane + 128] = jnp.concatenate(two, axis=0).astype(BF)

    loads[0].wait()
    loads[3].wait()
    ti = lax.broadcasted_iota(jnp.int32, (128, 16), 0) // 8
    tj = lax.broadcasted_iota(jnp.int32, (128, 16), 1)
    pick = (ti == tj).astype(BF)
    spread = jnp.dot(pick, mix_ref[...], preferred_element_type=F32).astype(BF)
    spread = lax.dot_general(spread, pick, NEG, preferred_element_type=F32)
    ri = lax.broadcasted_iota(jnp.int32, (128, 128), 0) % 8
    rj = lax.broadcasted_iota(jnp.int32, (128, 128), 1) % 8
    mix = jnp.where(ri == rj, spread, 0.0).astype(BF)

    def embed(h):
        rows = slice(h * 256, h * 256 + 256)
        summed = jnp.dot(tok[rows, :], embed_v[...], preferred_element_type=F32)
        wide = summed.reshape(2, 16, 8, 1024) + pos_ref[...].astype(F32)[None, :, None, :]
        tokens_v[rows, :] = wide.reshape(256, 1024).astype(BF)

    def mixes(h):
        for pi in (2 * h, 2 * h + 1):
            rows = slice(pi * 128, pi * 128 + 128)
            wide = tokens_v[rows, :].astype(F32)
            mixing = jnp.dot(mix, norm(wide).astype(BF), preferred_element_type=F32)
            mixed = (wide + mixing).astype(BF)
            tokens_v[rows, :] = mixed
            normed_v[rows, :] = norm(mixed.astype(F32)).astype(BF)

    def widen(h, n):
        rows = slice(h * 256, h * 256 + 256)
        lanes = pl.ds(pl.multiple_of(n * 1024, 1024), 1024)
        hidden = jnp.dot(normed_v[rows, :], up_v[:, lanes], preferred_element_type=F32)
        hidden_v[rows, lanes] = gelu(hidden)

    def narrow(h):
        rows = slice(h * 256, h * 256 + 256)
        summed = jnp.dot(hidden_v[rows, :], down_v[...], preferred_element_type=F32)
        encoded = norm(tokens_v[rows, :].astype(F32) + summed)
        total = jnp.sum(encoded.reshape(2, 16, 8, 1024), axis=1)
        pooled_v[h * 16:h * 16 + 16, :] = total.reshape(16, 1024) * 0.0625

    gather(0)
    embed(0)
    gather(1)
    embed(1)
    mixes(0)
    loads[1].wait()
    loads[2].start()
    feat_copy.start()
    widen(0, 0)
    mixes(1)

    @pl.loop(1, 4, unroll=3)
    def _(n):
        widen(0, n)

    @pl.loop(0, 4, unroll=4)
    def _(n):
        widen(1, n)

    loads[2].wait()
    narrow(0)
    narrow(1)

    for load in loads[4:]:
        load.wait()
    sc_v[0, :, 0:8] = lax.dot_general(
        pooled_v[...].astype(BF), head_ref[...], NEG, preferred_element_type=F32
    )
    for s in range(32):
        line = sc_v[0, pl.ds(patch_ref[0, 0, s], 1), :]
        sc_v[1, pl.ds(s, 1), :] = jnp.where(s < count_ref[0, 0], line, 0.0)
    score_ref[...] = jnp.transpose(sc_v[1], (1, 0))[0:8]
    feat_copy.wait()


def classify(f4, embed, patch, count, pos, mix, head, up, down):
    vm = pl.BlockSpec(memory_space=pltpu.VMEM)
    hb = pl.BlockSpec(memory_space=pltpu.HBM)
    return pl.pallas_call(
        token_kernel,
        out_shape=(
            jax.ShapeDtypeStruct((64, 128, 128), BF),
            jax.ShapeDtypeStruct((8, 32), F32),
        ),
        in_specs=[vm, vm, pl.BlockSpec(memory_space=pltpu.SMEM)] + [hb] * 6,
        out_specs=(hb, vm),
        scratch_shapes=[
            pltpu.SMEM((1, 1, 32), jnp.int32),
            pltpu.VMEM((16, 1024), BF),
            pltpu.VMEM((16, 16), BF),
            pltpu.VMEM((8, 1024), BF),
            pltpu.VMEM((64, 128, 128), BF),
            pltpu.VMEM((512, 2048), BF),
            pltpu.VMEM((1024, 4096), BF),
            pltpu.VMEM((4096, 1024), BF),
            pltpu.VMEM((512, 1024), BF),
            pltpu.VMEM((512, 1024), BF),
            pltpu.VMEM((512, 4096), BF),
            pltpu.VMEM((32, 1024), F32),
            pltpu.VMEM((2, 32, 128), F32),
            pltpu.SemaphoreType.DMA((6,)),
            pltpu.SemaphoreType.DMA,
        ],
        compiler_params=pltpu.CompilerParams(vmem_limit_bytes=40 * 2**20),
        name="classify",
    )(f4, embed, count, *in_hbm(patch, pos, mix, head, up, down))


def in_hbm(*arrays):
    return tuple(pltpu.with_memory_space_constraint(a, pltpu.HBM) for a in arrays)


def on_device(input_field, conv_first, conv_rest, flag_patch, flag_count, w_embed, pos_embed,
              token_mix, w_up, w_down, w_head):
    f4, embed = convolve(
        input_field, jnp.transpose(conv_first, (0, 1, 3, 2)).reshape(9, 64, 128),
        conv_rest.reshape(27, 128, 128), w_embed,
    )
    features, scores = classify(
        f4, embed, flag_patch, flag_count, pos_embed, token_mix, w_head.T, w_up, w_down,
    )
    return (features, scores.T[None, None])


def solution(mesh):
    placed = (
        P(None, "lat", "lon"), P(), P(), P("lat", "lon", None), P("lat", "lon"),
        P(), P(), P(), P(), P(), P(),
    )
    return jax.shard_map(
        on_device,
        mesh=mesh,
        in_specs=placed,
        out_specs=(P("lat", "lon", None), P("lat", "lon", None, None)),
        check_vma=False,
    )
```

```python
import functools

import jax
import jax.numpy as jnp
from jax import lax
from jax.experimental import pallas as pl
from jax.experimental.pallas import tpu as pltpu
from jax.sharding import PartitionSpec as P

BF = jnp.bfloat16
F32 = jnp.float32
MESH = pl.DeviceIdType.MESH

W = 8
Q = W + 2
S = 16
COLS = W * S
STRIP = 40
HELD = 48
NEG = (((1,), (1,)), ((), ()))
POS = (((1,), (0,)), ((), ()))


def silu(v):
    half = 0.5 * v
    return half + half * jnp.tanh(half)


def gelu(v):
    v = v.astype(BF)
    half = BF(0.5) * v
    return half + half * jnp.tanh(v * (BF(0.7978845608028654) + BF(0.035677408136300125) * (v * v)))


def norm(v):
    centred = v - jnp.mean(v, axis=-1, keepdims=True)
    return centred * lax.rsqrt(jnp.mean(centred * centred, axis=-1, keepdims=True) + 1e-05)


def conv_kernel(x_hbm, first_hbm, rest_hbm, embed_hbm, f4, embed_v, x_ref, first_ref, rest_ref, xf, x0, x1, x2, x3, wt1, wm, we,
                colf, cornf, corner, col_l, col_r, sf0, sf1, sf2, sf3, r_right, r_left, r_br, r_bl, r_tr, r_tl,
                send_sem, recv_sem, load_sem):
    loads = [
        pltpu.make_async_copy(x_hbm, x_ref, load_sem.at[0]),
        pltpu.make_async_copy(first_hbm, first_ref, load_sem.at[1]),
        pltpu.make_async_copy(rest_hbm, rest_ref, load_sem.at[2]),
        pltpu.make_async_copy(embed_hbm, embed_v, load_sem.at[3]),
    ]
    for load in loads[:3]:
        load.start()
    lon = lax.axis_index("lon")
    lat = lax.axis_index("lat")
    n_lon = lax.axis_size("lon")
    n_lat = lax.axis_size("lat")
    west = lax.rem(lon + n_lon - 1, n_lon)
    east = lax.rem(lon + 1, n_lon)
    north = lax.rem(lat + n_lat - 1, n_lat)
    south = lax.rem(lat + 1, n_lat)
    barrier = pltpu.get_barrier_semaphore()
    places = ((lon, north), (lon, south), (west, lat), (east, lat),
              (west, north), (east, north), (west, south), (east, south))
    to_north, to_south, level = (0, 4, 5), (1, 6, 7), (2, 3)
    has_north, has_south = lat > 0, lat < n_lat - 1

    def greet(those):
        for i in those:
            pl.semaphore_signal(barrier, inc=1, device_id=places[i], device_id_type=MESH)

    greet(level)
    pl.when(has_north)(lambda: greet(to_north))
    pl.when(has_south)(lambda: greet(to_south))
    low = jnp.where(lat == 0, 0, -64)
    high = jnp.where(lat == n_lat - 1, 64, 128)

    loads[0].wait()
    xf[...] = x_ref[...].astype(F32).reshape(64 * 64, 128)
    mm = lax.broadcasted_iota(jnp.int32, (Q * S, 128), 0)
    jj = lax.broadcasted_iota(jnp.int32, (Q * S, 128), 1)
    order = (jj == mm % S * W + mm // S - 1).astype(BF)

    def turn(k):
        rows = jnp.concatenate(
            [xf[pl.ds(2 * k + i, 64, 64), :] for i in range(4)], axis=0
        ).astype(BF)
        cells = lax.dot_general(order, rows, NEG, preferred_element_type=F32)
        for h in range(2):
            own = cells[:, h * 128:h * 128 + 128].reshape(Q, S, 128)
            x0[k + 2 + h] = own.astype(BF)
            for c in range(4):
                colf[0, c, pl.ds(k + h, 1), :] = own[c + 1, 0:1]
                colf[1, c, pl.ds(k + h, 1), :] = own[c + 5, 15:16]
            for c in range(2):
                sf0[0, 4 + c, pl.ds(k + 2 + h, 1), :] = own[c + 1, 0:1]
                sf0[1, c, pl.ds(k + 2 + h, 1), :] = own[c + 7, 15:16]

    @pl.loop(0, 16, unroll=16)
    def _(k):
        turn(2 * k)

    cornf[...] = jnp.zeros((2, 2, 16, 128), F32)
    for e in range(2):
        for end in range(2):
            for c in range(4):
                cornf[e, end, 2 * c:2 * c + 2, :] = colf[e, c, 30 * end:30 * end + 2, :]
    corner[...] = cornf[...].astype(BF)
    col_l[...] = colf[0].astype(BF)
    col_r[...] = colf[1].astype(BF)

    loads[1].wait()
    loads[2].wait()
    loads[3].start()
    for ro in range(2):
        out = slice(ro * 128, ro * 128 + 128)
        for p in range(2):
            for dq in range(3):
                for half in range(2):
                    a = 2 * p + half - ro
                    at = (p * 3 + dq) * 2 + half
                    wt1[at * 64:at * 64 + 64, out] = (
                        first_ref[a * 3 + dq] if 0 <= a < 3 else jnp.zeros((64, 128), BF)
                    )
    for l in range(3):
        for o in range(2):
            out = slice(o * 128, o * 128 + 128)
            for dq in range(3):
                for i in range(2):
                    at = (dq * 2 + i) * 128
                    wm[l, out, at:at + 128] = rest_ref[l * 9 + (i + 1 - o) * 3 + dq]
            for e in range(2):
                for t in range(4):
                    b = t - o
                    we[l, e, out, t * 128:t * 128 + 128] = (
                        rest_ref[l * 9 + 6 * e + b] if 0 <= b < 3 else jnp.zeros((128, 128), BF)
                    )

    xs = (x0, x1, x2, x3)
    sfs = (sf0, sf1, sf2, sf3)

    def product(l, groups):
        def stack(p, first, step, *half):
            return jnp.concatenate(
                [get(p, c, *half) for get, n in groups for c in range(first, first + n, step)], axis=0
            )

        def split(whole, parts):
            at = 0
            for size, n in parts:
                yield [whole[at + c * size:at + c * size + size] for c in range(n)]
                at += size * n

        sizes = [(get(0, 0).shape[0], n) for get, n in groups]
        if l == 1:
            slabs = [stack(p, dq, 1) for p in range(2) for dq in range(3)]
            full = jnp.dot(jnp.concatenate(slabs, axis=1), wt1[...], preferred_element_type=F32)
            return list(split(full, sizes))
        slabs = []
        for dq in range(3):
            slabs += [stack(0, dq, 1, 1), stack(1, dq, 1, 0)]
        full = lax.dot_general(jnp.concatenate(slabs, axis=1), wm[l - 2], NEG, preferred_element_type=F32)
        outer = []
        for e in range(2):
            slabs = [stack(e, t, 2, e) for t in range(4)]
            part = lax.dot_general(
                jnp.concatenate(slabs, axis=1), we[l - 2, e], NEG, preferred_element_type=F32
            )
            outer.append(list(split(part, [(size, n // 2) for size, n in sizes])))
        sums = []
        for g, columns in enumerate(split(full, sizes)):
            for c in range(len(columns)):
                lanes = slice(c % 2 * 128, c % 2 * 128 + 128)
                columns[c] = columns[c] + jnp.concatenate(
                    [part[g][c // 2][:, lanes] for part in outer], axis=1
                )
            sums.append(columns)
        return sums

    def inside(l, first, shape, dim):
        pair = lax.broadcasted_iota(jnp.int32, shape, dim)
        lane = lax.broadcasted_iota(jnp.int32, shape, len(shape) - 1)
        row = l - 4 + 2 * (first + pair) + lane // 128
        return (row >= low) & (row < high)

    def of_main(l, k, r):
        src = xs[l - 1]

        def get(p, c, half=None):
            lanes = slice(None) if half is None else slice(half * 128, half * 128 + 128)
            part = src[pl.ds(k + p, r), c, :, lanes]
            return part.reshape(r * S, part.shape[-1])

        return get, W

    def keep(l, k, r, sums, border=False):
        for q in range(W):
            y = silu(sums[q]).reshape(r, S, 256)
            if border and l < 4:
                y = jnp.where(inside(l, k, (r, S, 256), 0), y, 0.0)
            if l == 4:
                for i in range(r):
                    for half in range(2):
                        f4[pl.ds((2 * (k + i) + half) * COLS + q, S, W), :] = (
                            y[i, :, half * 128:half * 128 + 128]
                        )
                continue
            dst = xs[l]
            dst[pl.ds(k, r), q + 1] = y.astype(BF)
            for i in range(r):
                if q == W - 1:
                    dst[k + i, 0] = pltpu.roll(y[i], 1, 0).astype(BF)
                if q == 0:
                    dst[k + i, W + 1] = pltpu.roll(y[i], S - 1, 0).astype(BF)
                for c in range(2):
                    if q == l + c:
                        sfs[l][0, 4 + c, pl.ds(k + i, 1), :] = y[i, 0:1]
                    if q == W - 2 - l + c:
                        sfs[l][1, c, pl.ds(k + i, 1), :] = y[i, S - 1:S]

    def inner(l, r, first=0, last=None):
        pairs = 32 - l
        steps = (pairs + r - 1) // r

        @pl.loop(first, steps if last is None else last)
        def _(step):
            k = jnp.minimum(2 + step * r, 2 + pairs - r)
            keep(l, k, r, product(l, [of_main(l, k, r)])[0])

    inner(1, 16, 0, 1)

    surrounded = jnp.logical_and(has_north, has_south)
    pl.when(surrounded)(lambda: pl.semaphore_wait(barrier, 8))
    pl.when(jnp.logical_not(surrounded))(lambda: pl.semaphore_wait(barrier, 5))
    sends = (
        (x0.at[2:4, 1:W + 1], x0.at[34:36, 1:W + 1]), (x0.at[32:34, 1:W + 1], x0.at[0:2, 1:W + 1]),
        (col_l, r_right), (col_r, r_left), (corner.at[0, 0], r_br), (corner.at[1, 0], r_bl),
        (corner.at[0, 1], r_tr), (corner.at[1, 1], r_tl),
    )
    copies = []
    for i, ((src, dst), place) in enumerate(zip(sends, places)):
        copies.append(pltpu.make_async_remote_copy(
            src_ref=src, dst_ref=dst, send_sem=send_sem.at[i], recv_sem=recv_sem.at[i],
            device_id=place, device_id_type=MESH,
        ))

    def send(those):
        for i in those:
            copies[i].start()

    def sent(those):
        for i in those:
            copies[i].wait_send()

    def arrived(those):
        for i in those:
            copies[i].wait_recv()

    pl.when(has_north)(lambda: send(to_north))
    pl.when(has_south)(lambda: send(to_south))
    send(level)

    inner(1, 16, 1)
    inner(2, 15)
    inner(3, 15)
    inner(4, 14)

    loads[3].wait()
    sent(level)
    arrived(level)

    @pl.when(has_north)
    def _():
        sent(to_north)
        arrived(to_south)

    @pl.when(has_south)
    def _():
        sent(to_south)
        arrived(to_north)

    @pl.when(lat == 0)
    def _():
        x0[0:2] = jnp.zeros((2, Q, S, 128), BF)

    @pl.when(lat == n_lat - 1)
    def _():
        x0[34:36] = jnp.zeros((2, Q, S, 128), BF)

    sf0[0, 0:4, 2:34, :] = r_left[...].astype(F32)
    sf0[1, 2:6, 2:34, :] = r_right[...].astype(F32)
    for at, west_end, east_end in ((0, r_tl, r_tr), (34, r_bl, r_br)):
        for e, end in enumerate((west_end, east_end)):
            rows = end[...].astype(F32)
            for c in range(4):
                sf0[e, 2 * e + c, at:at + 2, :] = rows[2 * c:2 * c + 2]
        for k in (at, at + 1):
            first = x0[k, 1].astype(F32)
            last = x0[k, W].astype(F32)
            x0[k, 0] = pltpu.roll(last, 1, 0).astype(BF)
            x0[k, W + 1] = pltpu.roll(first, S - 1, 0).astype(BF)
            sf0[0, 4, k:k + 1, :] = first[0:1]
            sf0[0, 5, k:k + 1, :] = x0[k, 2].astype(F32)[0:1]
            sf0[1, 0, k:k + 1, :] = x0[k, W - 1].astype(F32)[S - 1:S]
            sf0[1, 1, k:k + 1, :] = last[S - 1:S]

    @pl.when(lat == 0)
    def _():
        sf0[:, :, 0:2, :] = jnp.zeros((2, 6, 2, 128), F32)

    @pl.when(lat == n_lat - 1)
    def _():
        sf0[:, :, 34:36, :] = jnp.zeros((2, 6, 2, 128), F32)

    def of_strips(l):
        src = sfs[l - 1]

        def get(p, c, half=None):
            lanes = slice(None) if half is None else slice(half * 128, half * 128 + 128)
            part = src[:, c, p:p + STRIP, lanes]
            return part.reshape(2 * STRIP, part.shape[-1]).astype(BF)

        return get, 4

    def keep_strips(l, sums):
        for c in range(4):
            y = silu(sums[c]).reshape(2, STRIP, 256)
            if l == 4:
                for side in range(2):
                    for half in range(2):
                        f4[pl.ds(half * COLS + 124 * side + c, 32, 2 * COLS), :] = (
                            y[side, 0:32, half * 128:half * 128 + 128]
                        )
                continue
            y = jnp.where(inside(l, 0, (1, STRIP, 256), 1), y, 0.0)
            for side in range(2):
                sfs[l][side, 2 * side + c, 0:STRIP, :] = y[side]

    for l in range(1, 5):
        top, bottom, sides = product(l, [of_main(l, 0, 2), of_main(l, 34 - l, 2), of_strips(l)])
        keep(l, 0, 2, top, True)
        keep(l, 34 - l, 2, bottom, True)
        keep_strips(l, sides)


def convolve(x, first, rest, embed):
    vm = pl.BlockSpec(memory_space=pltpu.VMEM)
    hb = pl.BlockSpec(memory_space=pltpu.HBM)
    side = pltpu.VMEM((4, 32, 128), BF)
    corner = pltpu.VMEM((16, 128), BF)
    return pl.pallas_call(
        conv_kernel,
        out_shape=(
            jax.ShapeDtypeStruct((64 * 128, 128), F32),
            jax.ShapeDtypeStruct((2048, 1024), BF),
        ),
        in_specs=[hb, hb, hb, hb],
        out_specs=(vm, vm),
        scratch_shapes=[
            pltpu.VMEM((64, 64, 128), BF),
            pltpu.VMEM((9, 64, 128), BF),
            pltpu.VMEM((27, 128, 128), BF),
            pltpu.VMEM((64 * 64, 128), F32),
            pltpu.VMEM((36, Q, S, 128), BF),
            pltpu.VMEM((35, Q, S, 256), BF),
            pltpu.VMEM((34, Q, S, 256), BF),
            pltpu.VMEM((33, Q, S, 256), BF),
            pltpu.VMEM((768, 256), BF),
            pltpu.VMEM((3, 256, 768), BF),
            pltpu.VMEM((3, 2, 256, 512), BF),
            pltpu.VMEM((2, 4, 32, 128), F32),
            pltpu.VMEM((2, 2, 16, 128), F32),
            pltpu.VMEM((2, 2, 16, 128), BF),
            side, side,
            pltpu.VMEM((2, 6, HELD, 128), F32),
            pltpu.VMEM((2, 6, HELD, 256), F32),
            pltpu.VMEM((2, 6, HELD, 256), F32),
            pltpu.VMEM((2, 6, HELD, 256), F32),
            side, side, corner, corner, corner, corner,
            pltpu.SemaphoreType.DMA((8,)),
            pltpu.SemaphoreType.DMA((8,)),
            pltpu.SemaphoreType.DMA((4,)),
        ],
        compiler_params=pltpu.CompilerParams(
            collective_id=0, has_side_effects=True, vmem_limit_bytes=40 * 2**20
        ),
        name="convolve",
    )(*in_hbm(x, first, rest, embed))


def token_kernel(f4, embed_v, count_ref, patch_hbm, pos_hbm, mix_hbm, head_hbm, up_hbm, down_hbm,
                 feat_hbm, score_ref, patch_ref, pos_ref, mix_ref, head_ref,
                 fo, tok, up_v, down_v, tokens_v, normed_v, hidden_v, pooled_v, sc_v, wsem, fsem):
    pairs = (
        (pos_hbm, pos_ref), (up_hbm, up_v), (down_hbm, down_v), (mix_hbm, mix_ref),
        (head_hbm, head_ref), (patch_hbm, patch_ref),
    )
    loads = [pltpu.make_async_copy(src, dst, wsem.at[i]) for i, (src, dst) in enumerate(pairs)]
    for i in (0, 3, 4, 5, 1):
        loads[i].start()
    feat_copy = pltpu.make_async_copy(fo, feat_hbm, fsem)

    def gather(h):
        for tr in range(8 * h, 8 * h + 8):
            for u in range(4):
                row = (tr * 4 + u) * COLS
                fo[tr * 4 + u] = f4[row:row + COLS, :].astype(BF)
                for b2 in range(2):
                    at = tr * 32 + b2 * 16
                    for v in range(4):
                        two = [f4[pl.ds(row + 4 * (2 * b2 + b) + v, 8, 16), :] for b in range(2)]
                        lane = (u * 4 + v) * 128
                        tok[at:at + 16, lane:lane + 128] = jnp.concatenate(two, axis=0).astype(BF)

    loads[0].wait()
    loads[3].wait()
    ti = lax.broadcasted_iota(jnp.int32, (128, 16), 0) // 8
    tj = lax.broadcasted_iota(jnp.int32, (128, 16), 1)
    pick = (ti == tj).astype(BF)
    spread = jnp.dot(pick, mix_ref[...], preferred_element_type=F32).astype(BF)
    spread = lax.dot_general(spread, pick, NEG, preferred_element_type=F32)
    ri = lax.broadcasted_iota(jnp.int32, (128, 128), 0) % 8
    rj = lax.broadcasted_iota(jnp.int32, (128, 128), 1) % 8
    mix = jnp.where(ri == rj, spread, 0.0).astype(BF)

    def embed(h):
        rows = slice(h * 256, h * 256 + 256)
        summed = jnp.dot(tok[rows, :], embed_v[...], preferred_element_type=F32)
        wide = summed.reshape(2, 16, 8, 1024) + pos_ref[...].astype(F32)[None, :, None, :]
        tokens_v[rows, :] = wide.reshape(256, 1024).astype(BF)

    def mixes(h):
        for pi in (2 * h, 2 * h + 1):
            rows = slice(pi * 128, pi * 128 + 128)
            wide = tokens_v[rows, :].astype(F32)
            mixing = jnp.dot(mix, norm(wide).astype(BF), preferred_element_type=F32)
            mixed = (wide + mixing).astype(BF)
            tokens_v[rows, :] = mixed
            normed_v[rows, :] = norm(mixed.astype(F32)).astype(BF)

    def widen(h, n):
        rows = slice(h * 256, h * 256 + 256)
        lanes = pl.ds(pl.multiple_of(n * 1024, 1024), 1024)
        hidden = jnp.dot(normed_v[rows, :], up_v[:, lanes], preferred_element_type=F32)
        hidden_v[rows, lanes] = gelu(hidden)

    def narrow(h):
        rows = slice(h * 256, h * 256 + 256)
        summed = jnp.dot(hidden_v[rows, :], down_v[...], preferred_element_type=F32)
        encoded = norm(tokens_v[rows, :].astype(F32) + summed)
        total = jnp.sum(encoded.reshape(2, 16, 8, 1024), axis=1)
        pooled_v[h * 16:h * 16 + 16, :] = total.reshape(16, 1024) * 0.0625

    gather(0)
    embed(0)
    gather(1)
    embed(1)
    mixes(0)
    loads[1].wait()
    loads[2].start()
    feat_copy.start()
    widen(0, 0)
    mixes(1)

    @pl.loop(1, 4, unroll=3)
    def _(n):
        widen(0, n)

    @pl.loop(0, 4, unroll=4)
    def _(n):
        widen(1, n)

    loads[2].wait()
    narrow(0)
    narrow(1)

    for load in loads[4:]:
        load.wait()
    sc_v[0, :, 0:8] = lax.dot_general(
        pooled_v[...].astype(BF), head_ref[...], NEG, preferred_element_type=F32
    )
    for s in range(32):
        line = sc_v[0, pl.ds(patch_ref[0, 0, s], 1), :]
        sc_v[1, pl.ds(s, 1), :] = jnp.where(s < count_ref[0, 0], line, 0.0)
    score_ref[...] = jnp.transpose(sc_v[1], (1, 0))[0:8]
    feat_copy.wait()


def classify(f4, embed, patch, count, pos, mix, head, up, down):
    vm = pl.BlockSpec(memory_space=pltpu.VMEM)
    hb = pl.BlockSpec(memory_space=pltpu.HBM)
    return pl.pallas_call(
        token_kernel,
        out_shape=(
            jax.ShapeDtypeStruct((64, 128, 128), BF),
            jax.ShapeDtypeStruct((8, 32), F32),
        ),
        in_specs=[vm, vm, pl.BlockSpec(memory_space=pltpu.SMEM)] + [hb] * 6,
        out_specs=(hb, vm),
        scratch_shapes=[
            pltpu.SMEM((1, 1, 32), jnp.int32),
            pltpu.VMEM((16, 1024), BF),
            pltpu.VMEM((16, 16), BF),
            pltpu.VMEM((8, 1024), BF),
            pltpu.VMEM((64, 128, 128), BF),
            pltpu.VMEM((512, 2048), BF),
            pltpu.VMEM((1024, 4096), BF),
            pltpu.VMEM((4096, 1024), BF),
            pltpu.VMEM((512, 1024), BF),
            pltpu.VMEM((512, 1024), BF),
            pltpu.VMEM((512, 4096), BF),
            pltpu.VMEM((32, 1024), F32),
            pltpu.VMEM((2, 32, 128), F32),
            pltpu.SemaphoreType.DMA((6,)),
            pltpu.SemaphoreType.DMA,
        ],
        compiler_params=pltpu.CompilerParams(vmem_limit_bytes=40 * 2**20),
        name="classify",
    )(f4, embed, count, *in_hbm(patch, pos, mix, head, up, down))


def in_hbm(*arrays):
    return tuple(pltpu.with_memory_space_constraint(a, pltpu.HBM) for a in arrays)


def on_device(input_field, conv_first, conv_rest, flag_patch, flag_count, w_embed, pos_embed,
              token_mix, w_up, w_down, w_head):
    f4, embed = convolve(
        input_field, jnp.transpose(conv_first, (0, 1, 3, 2)).reshape(9, 64, 128),
        conv_rest.reshape(27, 128, 128), w_embed,
    )
    features, scores = classify(
        f4, embed, flag_patch, flag_count, pos_embed, token_mix, w_head.T, w_up, w_down,
    )
    return (features, scores.T[None, None])


def solution(mesh):
    placed = (
        P(None, "lat", "lon"), P(), P(), P("lat", "lon", None), P("lat", "lon"),
        P(), P(), P(), P(), P(), P(),
    )
    return jax.shard_map(
        on_device,
        mesh=mesh,
        in_specs=placed,
        out_specs=(P("lat", "lon", None), P("lat", "lon", None, None)),
        check_vma=False,
    )
```
